256 devices in a mesh: blk: 16 (over z, x_lo), tp: 8 (over y, x_hi), grp: 2 (over core).
Axes of the slice: x: 4 (x_hi: 2, x_lo: 2; x = x_hi * 2 + x_lo), y: 4, z: 8, core: 2. Of those that a mesh axis runs over, the one named last changes fastest.
Arguments:
- queries: bfloat16 [2, 4096, 8192], P('grp', 'blk', 'tp'), may hold values from -48 to 48
- key_rows: bfloat16 [2, 4096, 1024], P('grp', 'blk', 'tp'), may hold values from -6 to 6
- value_rows: bfloat16 [2, 4096, 1024], P('grp', 'blk', 'tp'), may hold values from -6 to 6
- out_weight: bfloat16 [8192, 8192], P('tp', 'blk'), may hold values from -0.0625 to 0.0625
- lengths: int32 [2], P('grp'), may hold values from 1024 to 4096
Outputs:
- projected: bfloat16 [2, 4096, 8192], P('grp', 'blk', 'tp')
The draws below stay inside these ranges and needn't reach their ends.
All inputs are finite; a program needn't handle non-finite values.
Results may differ from the reference program's by a relative error of at most 0.017.
Values may be sent and summed in bfloat16 or wider, within the bound.
No kernel may reach another device: no remote copies, remote signals or barrier semaphores. Data moves between devices by JAX's collectives and lax.ppermute only.
A program may use at most 128 MiB of HBM per device.

```python
import math
import jax
import jax.numpy as jnp
from jax import lax

D = 8192
HQ = 64
HK = 8
HS = 128
SEQ = 4096
CONTEXTS = 2
N_TP = 8


def shared_fields(key):
    base_query = jnp.clip(jax.random.normal(jax.random.fold_in(key, 11), (CONTEXTS, SEQ, HQ * HS), jnp.float32), -6.0, 6.0)
    base_key = jnp.clip(jax.random.normal(jax.random.fold_in(key, 12), (CONTEXTS, SEQ, HK * HS), jnp.float32), -6.0, 6.0)
    return (base_query, base_key)


def draw_queries(key, part):
    base_query, base_key = shared_fields(key)
    return base_query.astype(jnp.bfloat16)


def draw_key_rows(key, part):
    base_query, base_key = shared_fields(key)
    return base_key.astype(jnp.bfloat16)


def shard_levels(own_key, extent, cuts, smallest, largest):
    def one(dim, parts):
        draws = jax.random.uniform(jax.random.fold_in(jax.random.fold_in(own_key, 6), dim), (parts,), jnp.float32, smallest / len(cuts), largest / len(cuts))
        return jnp.repeat(jnp.exp(draws), extent[dim] // parts).reshape((-1,) + (1,) * (len(extent) - dim - 1))

    loudness = one(*cuts[0])
    for cut in cuts[1:]:
        loudness = loudness * one(*cut)
    return loudness


def noise(rng, shape, scale, limit, pieces=(), kind=jnp.bfloat16):
    gain = shard_levels(rng, shape, pieces, -0.22, 0.18) if pieces else 1.0
    values = jax.random.normal(rng, shape, jnp.float32) * scale * gain
    return jnp.minimum(jnp.maximum(values, -limit), limit).astype(kind)


def setup_inputs(seed: int = 0) -> dict:
    key_of = jax.random.split(jax.random.key(seed), 6)
    queries = draw_queries(jax.random.fold_in(key_of[5], 71), 0)
    key_rows = draw_key_rows(jax.random.fold_in(key_of[5], 71), 0)
    value_rows = noise(key_of[2], (CONTEXTS, SEQ, HK * HS), 1.0, 6.0, ((0, 2), (1, 16), (2, 8)))
    out_weight = noise(key_of[3], (HQ * HS, D), (HQ * HS) ** -0.5, 0.0625, ((0, 8), (1, 16)))
    lengths = jax.random.randint(key_of[4], (CONTEXTS,), SEQ // 4, SEQ + 1).astype(jnp.int32)
    return dict(queries=queries, key_rows=key_rows, value_rows=value_rows, out_weight=out_weight, lengths=lengths)


def attend_context(query_rows, key_part, value_part, length):
    seq_len = query_rows.shape[0]
    groups = HQ // HK
    query_heads = query_rows.reshape(seq_len, HK, groups, HS)
    key_heads = key_part.reshape(seq_len, HK, HS).astype(jnp.float32)
    value_heads = value_part.reshape(seq_len, HK, HS).astype(jnp.float32)
    key_pos = jnp.arange(seq_len, dtype=jnp.int32)
    block_rows = math.gcd(seq_len, 256)

    def one_block(index):
        start_row = (index * block_rows).astype(jnp.int32)
        block = lax.dynamic_slice_in_dim(query_heads, start_row, block_rows, 0).astype(jnp.float32)
        scores = jnp.einsum("qkgd,rkd->kgqr", block, key_heads, precision=lax.Precision.HIGHEST) * (HS ** -0.5)
        query_pos = start_row + jnp.arange(block_rows, dtype=jnp.int32)
        visible = key_pos[None, :] <= query_pos[:, None]
        scores = jnp.where(visible, scores, -1e30)
        best_score = scores.max(-1, keepdims=True)
        weights = jnp.where(visible, jnp.exp(scores - best_score), 0.0)
        row_total = weights.sum(-1)
        rounded = lax.optimization_barrier(weights.astype(jnp.bfloat16)).astype(jnp.float32)
        mixed_values = jnp.einsum("kgqr,rkd->qkgd", rounded, value_heads, precision=lax.Precision.HIGHEST)
        result = mixed_values / jnp.transpose(row_total, (2, 0, 1))[..., None]
        result = jnp.where(query_pos[:, None, None, None] < length, result, 0.0)
        return result.reshape(block_rows, HQ * HS).astype(jnp.bfloat16)

    blocks = lax.map(one_block, jnp.arange(seq_len // block_rows, dtype=jnp.int32))
    return blocks.reshape(seq_len, HQ * HS)


def reference(queries, key_rows, value_rows, out_weight, lengths):
    outputs = []
    head_width = HQ * HS // N_TP
    for context in range(CONTEXTS):
        attended = attend_context(queries[context], key_rows[context], value_rows[context], lengths[context])
        summed = jnp.zeros((attended.shape[0], D), jnp.float32)
        for group in range(N_TP):
            part = jnp.dot(attended[:, group * head_width:(group + 1) * head_width],
                           out_weight[group * head_width:(group + 1) * head_width, :],
                           preferred_element_type=jnp.float32)
            part = lax.optimization_barrier(part.astype(jnp.bfloat16)).astype(jnp.float32)
            summed = summed + part
        outputs.append(summed.astype(jnp.bfloat16))
    return jnp.stack(outputs)
```

```python
import functools

import jax
import jax.numpy as jnp
from jax import lax
from jax.experimental import pallas as pl
from jax.experimental.pallas import tpu as pltpu
from jax.sharding import PartitionSpec as P

HS = 128
HEADS = 4
TOK = 256
PAIR = 2 * TOK
SLOTS = 8
SCALE_LOG2E = (HS ** -0.5) * 1.4426950408889634
VMEM_LIMIT = 22 * 1024 * 1024
WHOLE = pl.BlockSpec(memory_space=pltpu.VMEM)
ANYWHERE = pl.BlockSpec(memory_space=pl.ANY)
SCALARS = pl.BlockSpec(memory_space=pltpu.SMEM)


def attention_kernel(part, info_ref, q_ref, *rest):
    kv_refs = rest[:2 * SLOTS]
    out_ref, q_buf, k_buf, v_buf, s_buf, m_buf, acc_buf, sems, q_sem = rest[2 * SLOTS:]
    z = info_ref[0]
    x_lo = info_ref[1]
    first = info_ref[2]
    length = info_ref[3]

    def slot_copies(d, sources):
        copies = []
        for i, ref in enumerate(sources):
            rows = pl.ds(i * TOK, TOK)
            copies.append(pltpu.make_async_copy(ref.at[:, :HS], k_buf.at[d, rows, :], sems.at[d, i, 0]))
            copies.append(pltpu.make_async_copy(ref.at[:, HS:], v_buf.at[d, rows, :HS], sems.at[d, i, 1]))
        return copies

    @pl.when(first >= length)
    def _():
        out_ref[...] = jnp.zeros_like(out_ref)

    @pl.when(first < length)
    def _():
        width = HEADS * HS
        q_copy = pltpu.make_async_copy(q_ref.at[:, part * width:(part + 1) * width], q_buf, q_sem)
        q_copy.start()
        for d in range(SLOTS):
            @pl.when(d <= z)
            def _():
                for copy in slot_copies(d, kv_refs[2 * d:2 * d + 2]):
                    copy.start()

        v_buf[:, :, HS:] = jnp.ones((SLOTS, PAIR, HS), jnp.bfloat16)

        def arrive(d):
            for copy in slot_copies(d, kv_refs[:2]):
                copy.wait()

        def head_slice(h):
            return pl.ds(pl.multiple_of(h * HS, HS), HS)

        def score(h, j):
            return lax.dot_general(
                q_buf[:, head_slice(h)], k_buf[j], (((1,), (1,)), ((), ())),
                preferred_element_type=jnp.float32)

        def lane_max(s):
            top = s[:, :HS]
            for i in range(1, PAIR // HS):
                top = jnp.maximum(top, s[:, i * HS:(i + 1) * HS])
            return top

        def score_first(h):
            s = score(h, 0)
            row = lax.broadcasted_iota(jnp.int32, (TOK, PAIR), 0)
            col = lax.broadcasted_iota(jnp.int32, (TOK, PAIR), 1)
            seen = (col <= row) | ((col >= TOK) & (x_lo == 1))
            s = jnp.where(seen, s, -1e30)
            s_buf[h % 2, 0] = s
            return lane_max(s)

        def score_block(h, j, top):
            s = score(h, j)
            s_buf[h % 2, j] = s
            return jnp.maximum(top, lane_max(s))

        def finish_max(h, top):
            m_buf[h % 2] = jnp.broadcast_to(top.max(axis=-1, keepdims=True), (TOK, HS))

        def mix(h, j):
            m = m_buf[h % 2]
            wide = jnp.concatenate([m] * (PAIR // HS), axis=1)
            p = jnp.exp2((s_buf[h % 2, j] - wide) * SCALE_LOG2E)
            return jnp.dot(p.astype(jnp.bfloat16), v_buf[j], preferred_element_type=jnp.float32)

        def write_out(h):
            acc = acc_buf[...]
            row = lax.broadcasted_iota(jnp.int32, (TOK, HS), 0) + first
            o = acc[:, :HS] / acc[:, HS:]
            out_ref[:, head_slice(h)] = jnp.where(row < length, o, 0.0).astype(out_ref.dtype)

        q_copy.wait()
        arrive(0)

        def first_head(j, top):
            arrive(j)
            return score_block(0, j, top)

        top = lax.fori_loop(1, z + 1, first_head, score_first(0))
        finish_max(0, top)

        def head_step(h, carry):
            top = score_first(h)
            acc_buf[...] = mix(h - 1, 0)

            def both(j, t):
                acc_buf[...] += mix(h - 1, j)
                return score_block(h, j, t)

            top = lax.fori_loop(1, z + 1, both, top)
            finish_max(h, top)
            write_out(h - 1)
            return carry

        lax.fori_loop(1, HEADS, head_step, 0)
        acc_buf[...] = mix(HEADS - 1, 0)

        def last(j, carry):
            acc_buf[...] += mix(HEADS - 1, j)
            return carry

        lax.fori_loop(1, z + 1, last, 0)
        write_out(HEADS - 1)


def attention(part, info, q, blocks):
    width = HEADS * HS
    return pl.pallas_call(
        functools.partial(attention_kernel, part),
        out_shape=jax.ShapeDtypeStruct((TOK, width), jnp.bfloat16),
        in_specs=[SCALARS] + [ANYWHERE] * (1 + len(blocks)),
        out_specs=WHOLE,
        scratch_shapes=[
            pltpu.VMEM((TOK, width), jnp.bfloat16),
            pltpu.VMEM((SLOTS, PAIR, HS), jnp.bfloat16),
            pltpu.VMEM((SLOTS, PAIR, 2 * HS), jnp.bfloat16),
            pltpu.VMEM((2, SLOTS, TOK, PAIR), jnp.float32),
            pltpu.VMEM((2, TOK, HS), jnp.float32),
            pltpu.VMEM((TOK, 2 * HS), jnp.float32),
            pltpu.SemaphoreType.DMA((SLOTS, 2, 2)),
            pltpu.SemaphoreType.DMA,
        ],
        compiler_params=pltpu.CompilerParams(vmem_limit_bytes=VMEM_LIMIT),
        cost_estimate=pl.CostEstimate(flops=14_000_000_000, bytes_accessed=2 << 20, transcendentals=0),
        name="attention",
    )(info, q, *blocks)


def projection_kernel(targets, info_ref, *rest):
    halves = (rest[:5], rest[5:10])
    w_own, w_oth = rest[10:10 + SLOTS], rest[10 + SLOTS:10 + 2 * SLOTS]
    out_ref, a_buf, w_buf, sems = rest[10 + 2 * SLOTS:]
    z = info_ref[0]
    y = info_ref[4]
    x_hi = info_ref[5]
    places = [(r, e) for r in targets for e in range(2)]

    def pair(place, d):
        return (
            pltpu.make_async_copy(w_own[d], w_buf.at[place, 0], sems.at[place, 0]),
            pltpu.make_async_copy(w_oth[d], w_buf.at[place, 1], sems.at[place, 1]),
        )

    for place, (r, e) in enumerate(places):
        zz = lax.rem(y + r, 4) * 2 + lax.rem(x_hi + e, 2)
        need = lax.rem(z - zz + SLOTS, SLOTS)
        for d in range(SLOTS):
            @pl.when(need == d)
            def _():
                for copy in pair(place, d):
                    copy.start()

    for i, (a0, a1, a2_top, a2_low, a3) in enumerate(halves):
        width = a0.shape[1]
        left, right = pl.ds(i * width, width), pl.ds((2 + i) * width, width)
        a_buf[:TOK, left] = a0[...]
        a_buf[TOK:, left] = a1[...]
        a_buf[:TOK // 2, right] = a2_top[...]
        a_buf[TOK // 2:TOK, right] = a2_low[...]
        a_buf[TOK:, right] = a3[...]

    for place, _ in enumerate(places):
        for copy in pair(place, 0):
            copy.wait()
        w = jnp.concatenate([w_buf[place, 0], w_buf[place, 1]], axis=1)
        out = jnp.dot(a_buf[...], w, preferred_element_type=jnp.float32)
        out_ref[place] = out.astype(jnp.bfloat16)


def projection(targets, info, a_parts, w_own, w_oth):
    rows, cols = w_own[0].shape
    count = 2 * len(targets)
    return pl.pallas_call(
        functools.partial(projection_kernel, targets),
        out_shape=jax.ShapeDtypeStruct((count, PAIR, 2 * cols), jnp.bfloat16),
        in_specs=[SCALARS] + [WHOLE] * len(a_parts) + [ANYWHERE] * (2 * SLOTS),
        out_specs=WHOLE,
        scratch_shapes=[
            pltpu.VMEM((PAIR, rows), jnp.bfloat16),
            pltpu.VMEM((count, 2, rows, cols), jnp.bfloat16),
            pltpu.SemaphoreType.DMA((count, 2)),
        ],
        compiler_params=pltpu.CompilerParams(vmem_limit_bytes=VMEM_LIMIT),
        cost_estimate=pl.CostEstimate(
            flops=count * 800_000_000, bytes_accessed=count << 20, transcendentals=0),
        name="projection",
    )(info, *a_parts, *w_own, *w_oth)


def assemble_kernel(info_ref, p0, p1, p2, p3, out_ref):
    x_lo = info_ref[1]
    x_hi = info_ref[5]
    g = info_ref[6]
    for rel, ref in enumerate((p0, p1, p2, p3)):
        src_lo = lax.rem(x_lo + (rel & 1), 2)
        src_hi = lax.rem(x_hi + (rel >> 1), 2)
        base = ((1 - src_lo) * 2 + src_hi) * 256
        for k in range(2):
            at = base + lax.rem(g + k, 2) * HS
            out_ref[:, pl.ds(pl.multiple_of(at, HS), HS)] = ref[:, k * HS:(k + 1) * HS]


def assemble(info, pieces):
    return pl.pallas_call(
        assemble_kernel,
        out_shape=jax.ShapeDtypeStruct((TOK, 4 * pieces[0].shape[1]), jnp.bfloat16),
        in_specs=[SCALARS] + [WHOLE] * 4,
        out_specs=WHOLE,
        compiler_params=pltpu.CompilerParams(vmem_limit_bytes=VMEM_LIMIT),
        name="assemble",
    )(info, *pieces)


def after(value, *others):
    return lax.optimization_barrier((value, *others))[0]


def local(queries, key_rows, value_rows, out_weight, lengths):
    blk = lax.axis_index("blk")
    tp = lax.axis_index("tp")
    g = lax.axis_index("grp")
    z, x_lo = blk // 2, blk % 2
    y, x_hi = tp // 2, tp % 2
    info = jnp.stack([z, x_lo, blk * TOK, lengths[0], y, x_hi, g, jnp.zeros_like(g)]).astype(jnp.int32)

    def z_shift(value, step):
        return lax.ppermute(value, "blk", [(i, (i + 2 * step) % 16) for i in range(16)])

    def y_shift(value, step):
        return lax.ppermute(value, "tp", [(i, (i + 2 * step) % 8) for i in range(8)])

    def x_flip(value, rel):
        if rel == 1:
            return lax.ppermute(value, "blk", [(i, i ^ 1) for i in range(16)])
        if rel == 2:
            return lax.ppermute(value, "tp", [(i, i ^ 1) for i in range(8)])
        return lax.ppermute(value, ("blk", "tp"), [(i, i ^ 9) for i in range(128)])

    own_kv = jnp.concatenate([key_rows[0], value_rows[0]], axis=1)
    up1, dn1 = z_shift(own_kv, 1), z_shift(own_kv, -1)
    up2, dn2 = z_shift(up1, 1), z_shift(dn1, -1)
    up3, dn3 = z_shift(up2, 1), z_shift(dn2, -1)
    up4 = z_shift(up3, 1)
    blocks = []
    for mine in (own_kv, up1, up2, up3, up4, dn3, dn2, dn1):
        blocks += [mine, x_flip(mine, 1)]

    quarter = out_weight.shape[1] // 4
    give1 = lax.dynamic_slice_in_dim(out_weight, (x_hi * 2 + g) * quarter, quarter, 1)
    give3 = lax.dynamic_slice_in_dim(out_weight, ((1 - x_hi) * 2 + g) * quarter, quarter, 1)
    give1, give3 = after(give1, up1), after(give3, up1)
    w0 = jnp.concatenate([x_flip(give1, 1), x_flip(give3, 3)], axis=0)
    w0 = after(w0, dn3)
    rows = w0.shape[0] // 2
    w_up1, w_dn1 = z_shift(w0, 1), z_shift(w0, -1)

    def swap(w):
        return lax.ppermute(w, "grp", [(0, 1), (1, 0)])

    o0 = swap(w0)
    att0 = after(attention(0, info, queries[0], blocks), o0)
    w_up2, w_dn2 = z_shift(after(w_up1, att0), 1), z_shift(after(w_dn1, att0), -1)
    o_up1, o_dn1 = swap(w_up1), swap(w_dn1)
    att1 = attention(1, info, queries[0], [after(blocks[0], att0)] + blocks[1:])
    near0 = x_flip(att0, 1), x_flip(att0, 3)
    att1 = after(att1, *near0, o_up1, o_dn1)
    near1 = x_flip(att1, 1), x_flip(att1, 3)

    half = TOK // 2

    def x_gather(a, a1, a3):
        return a, a1, x_flip(a3[:half], 1), x_flip(a1[half:], 3), a3

    a_parts = x_gather(att0, *near0) + x_gather(att1, *near1)
    w_up3, w_dn3 = z_shift(after(w_up2, att1), 1), z_shift(after(w_dn2, att1), -1)
    w_up4, w_dn4 = z_shift(w_up3[:rows], 1), z_shift(w_dn3[rows:], -1)
    w4 = jnp.concatenate([w_up4, w_dn4], axis=0)
    w_slots = [w0, w_up1, w_up2, w_up3, w4, w_dn3, w_dn2, w_dn1]
    w_other = [o0, o_up1, swap(w_up2), swap(w_up3), swap(w4), swap(w_dn3), swap(w_dn2), o_dn1]

    f32 = jnp.float32
    far = projection((2,), info, a_parts, w_slots, w_other)
    from_up_2a, from_dn_2b = y_shift(far[0], 1), y_shift(far[1], -1)
    near = projection((1, 3), info, a_parts, w_slots, w_other)
    up_b, dn_a = y_shift(near[1], 1), y_shift(near[2], -1)
    up_a = y_shift((near[0].astype(f32) + from_up_2a.astype(f32)).astype(jnp.bfloat16), 1)
    dn_b = y_shift((near[3].astype(f32) + from_dn_2b.astype(f32)).astype(jnp.bfloat16), -1)
    mine = projection((0,), info, a_parts, w_slots, w_other)

    def total(own, up, dn):
        return (own.astype(f32) + up.astype(f32) + dn.astype(f32)).astype(jnp.bfloat16)

    same_hi = total(mine[0], up_a, dn_a)
    other_hi = total(mine[1], up_b, dn_b)
    pieces = (same_hi[:TOK], x_flip(same_hi[TOK:], 1), x_flip(other_hi[:TOK], 2), x_flip(other_hi[TOK:], 3))
    return assemble(info, pieces)[None]


def solution(mesh):
    in_specs = (
        P("grp", "blk", "tp"),
        P("grp", "blk", "tp"),
        P("grp", "blk", "tp"),
        P("tp", "blk"),
        P("grp"),
    )
    out_specs = P("grp", "blk", "tp")
    return jax.shard_map(local, mesh=mesh, in_specs=in_specs, out_specs=out_specs, check_vma=False)
```

```python
import functools

import jax
import jax.numpy as jnp
from jax import lax
from jax.experimental import pallas as pl
from jax.experimental.pallas import tpu as pltpu
from jax.sharding import PartitionSpec as P

HS = 128
TOK = 256
HEADS = 8
PAIR = 2 * TOK
SLOTS = 8
ROWS = 512
SCALE_LOG2E = (HS ** -0.5) * 1.4426950408889634
VMEM_LIMIT = 16 * 1024 * 1024
WHOLE = pl.BlockSpec(memory_space=pltpu.VMEM)
ANYWHERE = pl.BlockSpec(memory_space=pl.ANY)
SCALARS = pl.BlockSpec(memory_space=pltpu.SMEM)


def attention_kernel(base, heads, sources, info_ref, q_ref, *rest):
    kv_count = len(rest) - 9
    kv_refs = rest[:kv_count]
    out_ref, q_buf, k_buf, v_buf, s_buf, m_buf, acc_buf, sems, q_sems = rest[kv_count:]
    z = info_ref[0]
    x_lo = info_ref[1]
    first = info_ref[2]
    length = info_ref[3]

    def slot_copies(d):
        copies = []
        for i, (which, at) in enumerate(sources[d]):
            ref = kv_refs[which]
            rows = pl.ds(i * TOK, TOK)
            copies.append(pltpu.make_async_copy(
                ref.at[at:at + TOK, :HS], k_buf.at[d, rows, :], sems.at[d, i, 0]))
            copies.append(pltpu.make_async_copy(
                ref.at[at:at + TOK, HS:], v_buf.at[d, rows, :HS], sems.at[d, i, 1]))
        return copies

    def arrive(d):
        for i in range(2):
            rows = pl.ds(i * TOK, TOK)
            ref = kv_refs[0]
            pltpu.make_async_copy(ref.at[:, :HS], k_buf.at[d, rows, :], sems.at[d, i, 0]).wait()
            pltpu.make_async_copy(ref.at[:, HS:], v_buf.at[d, rows, :HS], sems.at[d, i, 1]).wait()

    @pl.when(first >= length)
    def _():
        out_ref[...] = jnp.zeros_like(out_ref)

    @pl.when(first < length)
    def _():
        q_copies = []
        for h in range(heads):
            at = (base + h) * HS
            q_copies.append(pltpu.make_async_copy(
                q_ref.at[:, at:at + HS], q_buf.at[pl.ds(h * TOK, TOK), :], q_sems.at[h]))
            q_copies[-1].start()
        for d in range(SLOTS):
            @pl.when(d <= z)
            def _():
                for copy in slot_copies(d):
                    copy.start()

        v_buf[:, :, HS:] = jnp.ones((SLOTS, PAIR, HS), jnp.bfloat16)

        def score(t, j):
            return lax.dot_general(
                q_buf[t * ROWS:(t + 1) * ROWS, :], k_buf[j], (((1,), (1,)), ((), ())),
                preferred_element_type=jnp.float32)

        def lane_max(s):
            top = s[:, :HS]
            for i in range(1, PAIR // HS):
                top = jnp.maximum(top, s[:, i * HS:(i + 1) * HS])
            return top

        def score_first(t):
            s = score(t, 0)
            row = lax.broadcasted_iota(jnp.int32, (ROWS, PAIR), 0) & (TOK - 1)
            col = lax.broadcasted_iota(jnp.int32, (ROWS, PAIR), 1)
            seen = (col <= row) | ((col >= TOK) & (x_lo == 1))
            s = jnp.where(seen, s, -1e30)
            s_buf[0] = s
            m_buf[t % 2] = lane_max(s)

        def score_block(t, j):
            s = score(t, j)
            s_buf[j] = s
            m_buf[t % 2] = jnp.maximum(m_buf[t % 2], lane_max(s))

        def finish_max(t):
            m_buf[t % 2] = jnp.broadcast_to(m_buf[t % 2].max(axis=-1, keepdims=True), (ROWS, HS))

        def mix(t, j):
            wide = jnp.concatenate([m_buf[t % 2]] * (PAIR // HS), axis=1)
            p = jnp.exp2((s_buf[j] - wide) * SCALE_LOG2E)
            return jnp.dot(p.astype(jnp.bfloat16), v_buf[j], preferred_element_type=jnp.float32)

        def write_out(t):
            acc = acc_buf[...]
            row = (lax.broadcasted_iota(jnp.int32, (ROWS, HS), 0) & (TOK - 1)) + first
            o = jnp.where(row < length, acc[:, :HS] / acc[:, HS:], 0.0).astype(out_ref.dtype)
            for i in range(ROWS // TOK):
                h = t * (ROWS // TOK) + i
                out_ref[:, h * HS:(h + 1) * HS] = o[i * TOK:(i + 1) * TOK]

        for copy in q_copies:
            copy.wait()
        tiles = heads * TOK // ROWS
        for t in range(tiles + 1):
            if t == 0:
                arrive(0)
            if t > 0:
                acc_buf[...] = mix(t - 1, 0)
            if t < tiles:
                score_first(t)

            def step(j, carry):
                if t == 0:
                    arrive(j)
                if t > 0:
                    acc_buf[...] += mix(t - 1, j)
                if t < tiles:
                    score_block(t, j)
                return carry

            lax.fori_loop(1, z + 1, step, 0)
            if t < tiles:
                finish_max(t)
            if t > 0:
                write_out(t - 1)


def attention(base, heads, info, q, sources, blocks):
    width = heads * HS
    return pl.pallas_call(
        functools.partial(attention_kernel, base, heads, sources),
        out_shape=jax.ShapeDtypeStruct((TOK, width), jnp.bfloat16),
        in_specs=[SCALARS] + [ANYWHERE] * (1 + len(blocks)),
        out_specs=WHOLE,
        scratch_shapes=[
            pltpu.VMEM((heads * TOK, HS), jnp.bfloat16),
            pltpu.VMEM((SLOTS, PAIR, HS), jnp.bfloat16),
            pltpu.VMEM((SLOTS, PAIR, 2 * HS), jnp.bfloat16),
            pltpu.VMEM((SLOTS, ROWS, PAIR), jnp.float32),
            pltpu.VMEM((2, ROWS, HS), jnp.float32),
            pltpu.VMEM((ROWS, 2 * HS), jnp.float32),
            pltpu.SemaphoreType.DMA((SLOTS, 2, 2)),
            pltpu.SemaphoreType.DMA((heads,)),
        ],
        compiler_params=pltpu.CompilerParams(vmem_limit_bytes=VMEM_LIMIT),
        cost_estimate=pl.CostEstimate(flops=heads * 3_500_000_000, bytes_accessed=2 << 20, transcendentals=0),
        name="attention",
    )(info, q, *blocks)


def projection_kernel(targets, build, info_ref, *rest):
    count = 2 * len(targets)
    inputs = 8 if build else 1
    parts, rest = rest[:inputs], rest[inputs:]
    w_own, w_oth, rest = rest[:SLOTS], rest[SLOTS:2 * SLOTS], rest[2 * SLOTS:]
    outs, rest = rest[:count], rest[count:]
    if build:
        a_buf, w_buf, sems = rest
    else:
        (a_buf,) = parts
        w_buf, sems = rest
    z = info_ref[0]
    y = info_ref[4]
    x_hi = info_ref[5]
    places = [(r, e) for r in targets for e in range(2)]

    def pair(place, d):
        return (
            pltpu.make_async_copy(w_own[d], w_buf.at[place, 0], sems.at[place, 0]),
            pltpu.make_async_copy(w_oth[d], w_buf.at[place, 1], sems.at[place, 1]),
        )

    for place, (r, e) in enumerate(places):
        zz = lax.rem(y + r, 4) * 2 + lax.rem(x_hi + e, 2)
        need = lax.rem(z - zz + SLOTS, SLOTS)
        for d in range(SLOTS):
            @pl.when(need == d)
            def _():
                for copy in pair(place, d):
                    copy.start()

    if build:
        att0, near1, near3, att1, mix1, mix3, top, bottom = parts
        half, cut = TOK // 2, att0.shape[1]
        wide = HEADS * HS
        a_buf[:TOK, :cut] = att0[...]
        a_buf[:TOK, cut:wide] = att1[...]
        a_buf[TOK:, :cut] = near1[...]
        a_buf[TOK:, cut:wide] = mix1[:TOK]
        a_buf[TOK:, wide:wide + cut] = near3[...]
        a_buf[TOK:, wide + cut:] = mix3[:TOK]
        a_buf[:half, wide:wide + cut] = mix1[TOK:]
        a_buf[half:TOK, wide:wide + cut] = mix3[TOK:]
        a_buf[:half, wide + cut:] = top[...]
        a_buf[half:TOK, wide + cut:] = bottom[...]

    for place, _ in enumerate(places):
        for copy in pair(place, 0):
            copy.wait()
        w = jnp.concatenate([w_buf[place, 0], w_buf[place, 1]], axis=1)
        out = jnp.dot(a_buf[...], w, preferred_element_type=jnp.float32)
        outs[place][...] = out.astype(jnp.bfloat16)


def projection(targets, info, a_parts, weights):
    rows, cols = weights[0].shape
    count = 2 * len(targets)
    build = len(a_parts) > 1
    shapes = [jax.ShapeDtypeStruct((PAIR, 2 * cols), jnp.bfloat16)] * count
    if build:
        shapes.append(jax.ShapeDtypeStruct((PAIR, rows), jnp.bfloat16))
    return pl.pallas_call(
        functools.partial(projection_kernel, targets, build),
        out_shape=shapes,
        in_specs=[SCALARS] + [WHOLE] * len(a_parts) + [ANYWHERE] * len(weights),
        out_specs=[WHOLE] * len(shapes),
        scratch_shapes=[
            pltpu.VMEM((count, 2, rows, cols), jnp.bfloat16),
            pltpu.SemaphoreType.DMA((count, 2)),
        ],
        compiler_params=pltpu.CompilerParams(vmem_limit_bytes=VMEM_LIMIT),
        cost_estimate=pl.CostEstimate(
            flops=count * 800_000_000, bytes_accessed=count << 20, transcendentals=0),
        name="projection",
    )(info, *a_parts, *weights)


def assemble_kernel(info_ref, p0, p1, p2, p3, out_ref):
    x_lo = info_ref[1]
    x_hi = info_ref[5]
    g = info_ref[6]
    for rel, ref in enumerate((p0, p1, p2, p3)):
        src_lo = lax.rem(x_lo + (rel & 1), 2)
        src_hi = lax.rem(x_hi + (rel >> 1), 2)
        base = ((1 - src_lo) * 2 + src_hi) * 256
        for k in range(2):
            at = base + lax.rem(g + k, 2) * HS
            out_ref[:, pl.ds(pl.multiple_of(at, HS), HS)] = ref[:, k * HS:(k + 1) * HS]


def assemble(info, pieces):
    return pl.pallas_call(
        assemble_kernel,
        out_shape=jax.ShapeDtypeStruct((TOK, 4 * pieces[0].shape[1]), jnp.bfloat16),
        in_specs=[SCALARS] + [WHOLE] * 4,
        out_specs=WHOLE,
        compiler_params=pltpu.CompilerParams(vmem_limit_bytes=VMEM_LIMIT),
        name="assemble",
    )(info, *pieces)


def after(value, *others):
    return lax.optimization_barrier((value, *others))[0]


def local(queries, key_rows, value_rows, out_weight, lengths):
    blk = lax.axis_index("blk")
    tp = lax.axis_index("tp")
    g = lax.axis_index("grp")
    z, x_lo = blk // 2, blk % 2
    y, x_hi = tp // 2, tp % 2
    info = jnp.stack([z, x_lo, blk * TOK, lengths[0], y, x_hi, g, jnp.zeros_like(g)]).astype(jnp.int32)

    def z_shift(value, step):
        return lax.ppermute(value, "blk", [(i, (i + 2 * step) % 16) for i in range(16)])

    def y_shift(value, step):
        return lax.ppermute(value, "tp", [(i, (i + 2 * step) % 8) for i in range(8)])

    def x_flip(value, rel):
        if rel == 1:
            return lax.ppermute(value, "blk", [(i, i ^ 1) for i in range(16)])
        if rel == 2:
            return lax.ppermute(value, "tp", [(i, i ^ 1) for i in range(8)])
        return lax.ppermute(value, ("blk", "tp"), [(i, i ^ 9) for i in range(128)])

    def swap(value):
        return lax.ppermute(value, "grp", [(0, 1), (1, 0)])

    quarter = out_weight.shape[1] // 4
    keep_at, give_at = (x_hi * 2 + g) * quarter, ((1 - x_hi) * 2 + g) * quarter
    info, keep_at, give_at = lax.optimization_barrier(
        (info, keep_at.astype(jnp.uint32), give_at.astype(jnp.uint32)))

    own_kv = jnp.concatenate([key_rows[0], value_rows[0]], axis=1)
    own_kv = after(own_kv, info, keep_at, give_at)
    up1, dn1 = z_shift(own_kv, 1), z_shift(own_kv, -1)
    up2, dn2 = z_shift(up1, 1), z_shift(dn1, -1)
    up3, dn3 = z_shift(up2, 1), z_shift(dn2, -1)
    up4 = z_shift(up3, 1)
    blocks = []
    for mine in (own_kv, up1, up2, up3, up4, dn3, dn2, dn1):
        blocks += [mine, x_flip(mine, 1)]
    sources = tuple(((2 * d, 0), (2 * d + 1, 0)) for d in range(SLOTS))

    shape = (out_weight.shape[0], quarter)
    give1 = lax.dynamic_slice(out_weight, (jnp.uint32(0), keep_at), shape)
    give3 = lax.dynamic_slice(out_weight, (jnp.uint32(0), give_at), shape)
    give1, give3 = after(give1, up1), after(give3, up1)
    w0 = jnp.concatenate([x_flip(give1, 1), x_flip(give3, 3)], axis=0)
    w0 = after(w0, dn3)
    rows = w0.shape[0] // 2
    w_up1, w_dn1 = z_shift(w0, 1), z_shift(w0, -1)

    o0 = swap(w0)
    att0 = after(attention(0, 4, info, queries[0], sources, blocks), o0)
    w_up2, w_dn2 = z_shift(after(w_up1, att0), 1), z_shift(after(w_dn1, att0), -1)
    o_up1, o_dn1 = swap(w_up1), swap(w_dn1)
    near1, near3 = x_flip(att0, 1), x_flip(att0, 3)
    att1 = attention(4, 4, info, after(queries[0], att0), sources, blocks)
    half = TOK // 2
    att1 = after(att1, o_up1, o_dn1)
    send1 = jnp.concatenate([att1, near3[:half]], 0)
    send3 = jnp.concatenate([att1, near1[half:]], 0)
    mix1, mix3 = x_flip(send1, 1), x_flip(send3, 3)
    top, bottom = x_flip(mix3[:half], 1), x_flip(mix1[half:TOK], 3)
    a_parts = (att0, near1, near3, att1, mix1, mix3, top, bottom)

    w_up3, w_dn3 = z_shift(after(w_up2, send1, send3), 1), z_shift(after(w_dn2, send1, send3), -1)
    o_up2, o_dn2 = swap(w_up2), swap(w_dn2)
    w_up4 = z_shift(after(w_up3, mix1, mix3)[:rows], 1)
    w_dn4 = z_shift(after(w_dn3, mix1, mix3)[rows:], -1)
    w4 = jnp.concatenate([w_up4, w_dn4], axis=0)
    weights = (w0, w_up1, w_up2, w_up3, w4, w_dn3, w_dn2, w_dn1,
               o0, o_up1, o_up2, swap(w_up3), swap(w4), swap(w_dn3), o_dn2, o_dn1)

    f32 = jnp.float32
    c2a, c2b, a_full = projection((2,), info, a_parts, weights)
    up_2a, dn_2b = y_shift(c2a, 1), y_shift(c2b, -1)
    c1a, c1b, c3a, c3b = projection((1, 3), info, (a_full,), weights)
    up_b, dn_a = y_shift(c1b, 1), y_shift(c3a, -1)
    up_a = y_shift((c1a.astype(f32) + up_2a.astype(f32)).astype(jnp.bfloat16), 1)
    dn_b = y_shift((c3b.astype(f32) + dn_2b.astype(f32)).astype(jnp.bfloat16), -1)
    c0a, c0b = projection((0,), info, (a_full,), weights)

    def total(own, up, dn, at):
        rows = slice(at, at + TOK)
        return (own[rows].astype(f32) + up[rows].astype(f32) + dn[rows].astype(f32)).astype(jnp.bfloat16)

    pieces = (
        total(c0a, up_a, dn_a, 0),
        x_flip(total(c0a, up_a, dn_a, TOK), 1),
        x_flip(total(c0b, up_b, dn_b, 0), 2),
        x_flip(total(c0b, up_b, dn_b, TOK), 3),
    )
    return assemble(info, pieces)[None]


def solution(mesh):
    in_specs = (
        P("grp", "blk", "tp"),
        P("grp", "blk", "tp"),
        P("grp", "blk", "tp"),
        P("tp", "blk"),
        P("grp"),
    )
    out_specs = P("grp", "blk", "tp")
    return jax.shard_map(local, mesh=mesh, in_specs=in_specs, out_specs=out_specs, check_vma=False)
```

```python
import functools

import jax
import jax.numpy as jnp
from jax import lax
from jax.experimental import pallas as pl
from jax.experimental.pallas import tpu as pltpu
from jax.sharding import PartitionSpec as P

HS = 128
TOK = 256
HEADS = 8
PAIR = 2 * TOK
SLOTS = 8
ROWS = 512
SCALE_LOG2E = (HS ** -0.5) * 1.4426950408889634
VMEM_LIMIT = 16 * 1024 * 1024
WHOLE = pl.BlockSpec(memory_space=pltpu.VMEM)
ANYWHERE = pl.BlockSpec(memory_space=pl.ANY)
SCALARS = pl.BlockSpec(memory_space=pltpu.SMEM)


def attention_kernel(base, heads, sources, info_ref, q_ref, *rest):
    kv_count = len(rest) - 9
    kv_refs = rest[:kv_count]
    out_ref, q_buf, k_buf, v_buf, s_buf, m_buf, acc_buf, sems, q_sems = rest[kv_count:]
    z = info_ref[0]
    x_lo = info_ref[1]
    first = info_ref[2]
    length = info_ref[3]

    def slot_copies(d):
        copies = []
        for i, (which, at) in enumerate(sources[d]):
            ref = kv_refs[which]
            rows = pl.ds(i * TOK, TOK)
            copies.append(pltpu.make_async_copy(
                ref.at[at:at + TOK, :HS], k_buf.at[d, rows, :], sems.at[d, i, 0]))
            copies.append(pltpu.make_async_copy(
                ref.at[at:at + TOK, HS:], v_buf.at[d, rows, :HS], sems.at[d, i, 1]))
        return copies

    def arrive(d):
        for i in range(2):
            rows = pl.ds(i * TOK, TOK)
            ref = kv_refs[0]
            pltpu.make_async_copy(ref.at[:, :HS], k_buf.at[d, rows, :], sems.at[d, i, 0]).wait()
            pltpu.make_async_copy(ref.at[:, HS:], v_buf.at[d, rows, :HS], sems.at[d, i, 1]).wait()

    @pl.when(first >= length)
    def _():
        out_ref[...] = jnp.zeros_like(out_ref)

    @pl.when(first < length)
    def _():
        q_copies = []
        for h in range(heads):
            at = (base + h) * HS
            q_copies.append(pltpu.make_async_copy(
                q_ref.at[:, at:at + HS], q_buf.at[pl.ds(h * TOK, TOK), :], q_sems.at[h]))
            q_copies[-1].start()
        for d in range(SLOTS):
            @pl.when(d <= z)
            def _():
                for copy in slot_copies(d):
                    copy.start()

        v_buf[:, :, HS:] = jnp.ones((SLOTS, PAIR, HS), jnp.bfloat16)

        def score(t, j):
            return lax.dot_general(
                q_buf[t * ROWS:(t + 1) * ROWS, :], k_buf[j], (((1,), (1,)), ((), ())),
                preferred_element_type=jnp.float32)

        def lane_max(s):
            top = s[:, :HS]
            for i in range(1, PAIR // HS):
                top = jnp.maximum(top, s[:, i * HS:(i + 1) * HS])
            return top

        def score_first(t):
            s = score(t, 0)
            row = lax.broadcasted_iota(jnp.int32, (ROWS, PAIR), 0) & (TOK - 1)
            col = lax.broadcasted_iota(jnp.int32, (ROWS, PAIR), 1)
            seen = (col <= row) | ((col >= TOK) & (x_lo == 1))
            s = jnp.where(seen, s, -1e30)
            s_buf[0] = s
            m_buf[t % 2] = lane_max(s)

        def score_block(t, j):
            s = score(t, j)
            s_buf[j] = s
            m_buf[t % 2] = jnp.maximum(m_buf[t % 2], lane_max(s))

        def finish_max(t):
            m_buf[t % 2] = jnp.broadcast_to(m_buf[t % 2].max(axis=-1, keepdims=True), (ROWS, HS))

        def mix(t, j):
            wide = jnp.concatenate([m_buf[t % 2]] * (PAIR // HS), axis=1)
            p = jnp.exp2((s_buf[j] - wide) * SCALE_LOG2E)
            return jnp.dot(p.astype(jnp.bfloat16), v_buf[j], preferred_element_type=jnp.float32)

        def write_out(t):
            acc = acc_buf[...]
            row = (lax.broadcasted_iota(jnp.int32, (ROWS, HS), 0) & (TOK - 1)) + first
            o = jnp.where(row < length, acc[:, :HS] / acc[:, HS:], 0.0).astype(out_ref.dtype)
            for i in range(ROWS // TOK):
                h = t * (ROWS // TOK) + i
                out_ref[:, h * HS:(h + 1) * HS] = o[i * TOK:(i + 1) * TOK]

        for copy in q_copies:
            copy.wait()
        tiles = heads * TOK // ROWS
        for t in range(tiles + 1):
            if t == 0:
                arrive(0)
            if t > 0:
                acc_buf[...] = mix(t - 1, 0)
            if t < tiles:
                score_first(t)

            def step(j, carry):
                if t == 0:
                    arrive(j)
                if t > 0:
                    acc_buf[...] += mix(t - 1, j)
                if t < tiles:
                    score_block(t, j)
                return carry

            lax.fori_loop(1, z + 1, step, 0)
            if t < tiles:
                finish_max(t)
            if t > 0:
                write_out(t - 1)


def attention(base, heads, info, q, sources, blocks):
    width = heads * HS
    return pl.pallas_call(
        functools.partial(attention_kernel, base, heads, sources),
        out_shape=jax.ShapeDtypeStruct((TOK, width), jnp.bfloat16),
        in_specs=[SCALARS] + [ANYWHERE] * (1 + len(blocks)),
        out_specs=WHOLE,
        scratch_shapes=[
            pltpu.VMEM((heads * TOK, HS), jnp.bfloat16),
            pltpu.VMEM((SLOTS, PAIR, HS), jnp.bfloat16),
            pltpu.VMEM((SLOTS, PAIR, 2 * HS), jnp.bfloat16),
            pltpu.VMEM((SLOTS, ROWS, PAIR), jnp.float32),
            pltpu.VMEM((2, ROWS, HS), jnp.float32),
            pltpu.VMEM((ROWS, 2 * HS), jnp.float32),
            pltpu.SemaphoreType.DMA((SLOTS, 2, 2)),
            pltpu.SemaphoreType.DMA((heads,)),
        ],
        compiler_params=pltpu.CompilerParams(vmem_limit_bytes=VMEM_LIMIT),
        cost_estimate=pl.CostEstimate(flops=heads * 3_500_000_000, bytes_accessed=2 << 20, transcendentals=0),
        name="attention",
    )(info, q, *blocks)


def projection_kernel(targets, build, info_ref, *rest):
    count = 2 * len(targets)
    inputs = 8 if build else 1
    parts, rest = rest[:inputs], rest[inputs:]
    w_own, w_oth, rest = rest[:SLOTS], rest[SLOTS:2 * SLOTS], rest[2 * SLOTS:]
    outs, rest = rest[:count], rest[count:]
    if build:
        a_buf, w_buf, sems = rest
    else:
        (a_buf,) = parts
        w_buf, sems = rest
    z = info_ref[0]
    y = info_ref[4]
    x_hi = info_ref[5]
    places = [(r, e) for r in targets for e in range(2)]

    def pair(place, d):
        return (
            pltpu.make_async_copy(w_own[d], w_buf.at[place, 0], sems.at[place, 0]),
            pltpu.make_async_copy(w_oth[d], w_buf.at[place, 1], sems.at[place, 1]),
        )

    for place, (r, e) in enumerate(places):
        zz = lax.rem(y + r, 4) * 2 + lax.rem(x_hi + e, 2)
        need = lax.rem(z - zz + SLOTS, SLOTS)
        for d in range(SLOTS):
            @pl.when(need == d)
            def _():
                for copy in pair(place, d):
                    copy.start()

    if build:
        att0, near1, near3, att1, mix1, mix3, top, bottom = parts
        half, cut = TOK // 2, att0.shape[1]
        wide = HEADS * HS
        a_buf[:TOK, :cut] = att0[...]
        a_buf[:TOK, cut:wide] = att1[...]
        a_buf[TOK:, :cut] = near1[...]
        a_buf[TOK:, cut:wide] = mix1[:TOK]
        a_buf[TOK:, wide:wide + cut] = near3[...]
        a_buf[TOK:, wide + cut:] = mix3[:TOK]
        a_buf[:half, wide:wide + cut] = mix1[TOK:]
        a_buf[half:TOK, wide:wide + cut] = mix3[TOK:]
        a_buf[:half, wide + cut:] = top[...]
        a_buf[half:TOK, wide + cut:] = bottom[...]

    for place, _ in enumerate(places):
        for copy in pair(place, 0):
            copy.wait()
        w = jnp.concatenate([w_buf[place, 0], w_buf[place, 1]], axis=1)
        out = jnp.dot(a_buf[...], w, preferred_element_type=jnp.float32)
        outs[place][...] = out.astype(jnp.bfloat16)


def projection(targets, info, a_parts, weights):
    rows, cols = weights[0].shape
    count = 2 * len(targets)
    build = len(a_parts) > 1
    shapes = [jax.ShapeDtypeStruct((PAIR, 2 * cols), jnp.bfloat16)] * count
    if build:
        shapes.append(jax.ShapeDtypeStruct((PAIR, rows), jnp.bfloat16))
    return pl.pallas_call(
        functools.partial(projection_kernel, targets, build),
        out_shape=shapes,
        in_specs=[SCALARS] + [WHOLE] * len(a_parts) + [ANYWHERE] * len(weights),
        out_specs=[WHOLE] * len(shapes),
        scratch_shapes=[
            pltpu.VMEM((count, 2, rows, cols), jnp.bfloat16),
            pltpu.SemaphoreType.DMA((count, 2)),
        ],
        compiler_params=pltpu.CompilerParams(vmem_limit_bytes=VMEM_LIMIT),
        cost_estimate=pl.CostEstimate(
            flops=count * 800_000_000, bytes_accessed=count << 20, transcendentals=0),
        name="projection",
    )(info, *a_parts, *weights)


def assemble_kernel(info_ref, p0, p1, p2, p3, out_ref):
    x_lo = info_ref[1]
    x_hi = info_ref[5]
    g = info_ref[6]
    for rel, ref in enumerate((p0, p1, p2, p3)):
        src_lo = lax.rem(x_lo + (rel & 1), 2)
        src_hi = lax.rem(x_hi + (rel >> 1), 2)
        base = ((1 - src_lo) * 2 + src_hi) * 256
        for k in range(2):
            at = base + lax.rem(g + k, 2) * HS
            out_ref[:, pl.ds(pl.multiple_of(at, HS), HS)] = ref[:, k * HS:(k + 1) * HS]


def assemble(info, pieces):
    return pl.pallas_call(
        assemble_kernel,
        out_shape=jax.ShapeDtypeStruct((TOK, 4 * pieces[0].shape[1]), jnp.bfloat16),
        in_specs=[SCALARS] + [WHOLE] * 4,
        out_specs=WHOLE,
        compiler_params=pltpu.CompilerParams(vmem_limit_bytes=VMEM_LIMIT),
        name="assemble",
    )(info, *pieces)


def after(value, *others):
    return lax.optimization_barrier((value, *others))[0]


def local(queries, key_rows, value_rows, out_weight, lengths):
    blk = lax.axis_index("blk")
    tp = lax.axis_index("tp")
    g = lax.axis_index("grp")
    z, x_lo = blk // 2, blk % 2
    y, x_hi = tp // 2, tp % 2
    info = jnp.stack([z, x_lo, blk * TOK, lengths[0], y, x_hi, g, jnp.zeros_like(g)]).astype(jnp.int32)

    def z_shift(value, step):
        return lax.ppermute(value, "blk", [(i, (i + 2 * step) % 16) for i in range(16)])

    def y_shift(value, step):
        return lax.ppermute(value, "tp", [(i, (i + 2 * step) % 8) for i in range(8)])

    def x_flip(value, rel):
        if rel == 1:
            return lax.ppermute(value, "blk", [(i, i ^ 1) for i in range(16)])
        if rel == 2:
            return lax.ppermute(value, "tp", [(i, i ^ 1) for i in range(8)])
        return lax.ppermute(value, ("blk", "tp"), [(i, i ^ 9) for i in range(128)])

    def swap(value):
        return lax.ppermute(value, "grp", [(0, 1), (1, 0)])

    quarter = out_weight.shape[1] // 4
    keep_at, give_at = (x_hi * 2 + g) * quarter, ((1 - x_hi) * 2 + g) * quarter
    info, keep_at, give_at = lax.optimization_barrier(
        (info, keep_at.astype(jnp.uint32), give_at.astype(jnp.uint32)))

    own_kv = jnp.concatenate([key_rows[0], value_rows[0]], axis=1)
    own_kv = after(own_kv, info, keep_at, give_at)
    up1, dn1 = z_shift(own_kv, 1), z_shift(own_kv, -1)
    up2, dn2 = z_shift(up1, 1), z_shift(dn1, -1)
    up3, dn3 = z_shift(up2, 1), z_shift(dn2, -1)
    up4 = z_shift(up3, 1)
    blocks = []
    for mine in (own_kv, up1, up2, up3, up4, dn3, dn2, dn1):
        blocks += [mine, x_flip(mine, 1)]
    sources = tuple(((2 * d, 0), (2 * d + 1, 0)) for d in range(SLOTS))

    shape = (out_weight.shape[0], quarter)
    give1 = lax.dynamic_slice(out_weight, (jnp.uint32(0), keep_at), shape)
    give3 = lax.dynamic_slice(out_weight, (jnp.uint32(0), give_at), shape)
    give1, give3 = after(give1, up1), after(give3, up1)
    w0 = jnp.concatenate([x_flip(give1, 1), x_flip(give3, 3)], axis=0)
    w0 = after(w0, dn3)
    rows = w0.shape[0] // 2
    w_up1, w_dn1 = z_shift(w0, 1), z_shift(w0, -1)

    o0 = swap(w0)
    att0 = after(attention(0, 4, info, queries[0], sources, blocks), o0)
    w_up2, w_dn2 = z_shift(after(w_up1, att0), 1), z_shift(after(w_dn1, att0), -1)
    o_up1, o_dn1 = swap(w_up1), swap(w_dn1)
    near1, near3 = x_flip(att0, 1), x_flip(att0, 3)
    att1 = attention(4, 4, info, after(queries[0], att0), sources, blocks)
    half = TOK // 2
    att1 = after(att1, o_up1, o_dn1)
    send1 = jnp.concatenate([att1, near3[:half]], 0)
    send3 = jnp.concatenate([att1, near1[half:]], 0)
    mix1, mix3 = x_flip(send1, 1), x_flip(send3, 3)
    top, bottom = x_flip(mix3[:half], 1), x_flip(mix1[half:TOK], 3)
    a_parts = (att0, near1, near3, att1, mix1, mix3, top, bottom)

    w_up3, w_dn3 = z_shift(after(w_up2, send1, send3), 1), z_shift(after(w_dn2, send1, send3), -1)
    o_up2, o_dn2 = swap(w_up2), swap(w_dn2)
    w_up4 = z_shift(w_up3[:rows], 1)
    w_dn4 = z_shift(w_dn3[rows:], -1)
    w4 = jnp.concatenate([w_up4, w_dn4], axis=0)
    weights = (w0, w_up1, w_up2, w_up3, w4, w_dn3, w_dn2, w_dn1,
               o0, o_up1, o_up2, swap(w_up3), swap(w4), swap(w_dn3), o_dn2, o_dn1)

    f32 = jnp.float32
    c2s, c2f, a_full = projection((2,), info, a_parts, weights)
    up_2f, dn_2s = y_shift(c2f, 1), y_shift(c2s, -1)
    c1s, c1f, c3s, c3f = projection((1, 3), info, (a_full,), weights)
    up_f = y_shift((c1f.astype(f32) + up_2f.astype(f32)).astype(jnp.bfloat16), 1)
    dn_f = y_shift(c3f, -1)
    sum_s = (c3s.astype(f32) + dn_2s.astype(f32)).astype(jnp.bfloat16)
    up_s, dn_s = y_shift(after(c1s, sum_s), 1), y_shift(sum_s, -1)
    c0s, c0f = projection((0,), info, (a_full,), weights)

    def total(own, up, dn, at):
        rows = slice(at, at + TOK)
        return (own[rows].astype(f32) + up[rows].astype(f32) + dn[rows].astype(f32)).astype(jnp.bfloat16)

    pieces = (
        total(c0s, up_s, dn_s, 0),
        x_flip(total(c0s, up_s, dn_s, TOK), 1),
        x_flip(total(c0f, up_f, dn_f, 0), 2),
        x_flip(total(c0f, up_f, dn_f, TOK), 3),
    )
    return assemble(info, pieces)[None]


def solution(mesh):
    in_specs = (
        P("grp", "blk", "tp"),
        P("grp", "blk", "tp"),
        P("grp", "blk", "tp"),
        P("tp", "blk"),
        P("grp"),
    )
    out_specs = P("grp", "blk", "tp")
    return jax.shard_map(local, mesh=mesh, in_specs=in_specs, out_specs=out_specs, check_vma=False)
```

```python
import functools

import jax
import jax.numpy as jnp
from jax import lax
from jax.experimental import pallas as pl
from jax.experimental.pallas import tpu as pltpu
from jax.sharding import PartitionSpec as P

HS = 128
TOK = 256
HEADS = 8
PAIR = 2 * TOK
SLOTS = 8
ROWS = 512
SCALE_LOG2E = (HS ** -0.5) * 1.4426950408889634
VMEM_LIMIT = 16 * 1024 * 1024
WHOLE = pl.BlockSpec(memory_space=pltpu.VMEM)
ANYWHERE = pl.BlockSpec(memory_space=pl.ANY)
SCALARS = pl.BlockSpec(memory_space=pltpu.SMEM)


def attention_kernel(base, heads, keep, sources, info_ref, q_ref, *rest):
    if keep:
        kept_ref, rest = rest[0], rest[1:]
    kv_count = len(rest) - 9
    kv_refs = rest[:kv_count]
    out_ref, q_buf, k_buf, v_buf, s_buf, m_buf, acc_buf, sems, q_sems = rest[kv_count:]
    z = info_ref[0]
    x_lo = info_ref[1]
    first = info_ref[2]
    length = info_ref[3]

    def slot_copies(d):
        copies = []
        for i, (which, at) in enumerate(sources[d]):
            ref = kv_refs[which]
            rows = pl.ds(i * TOK, TOK)
            copies.append(pltpu.make_async_copy(
                ref.at[at:at + TOK, :HS], k_buf.at[d, rows, :], sems.at[d, i, 0]))
            copies.append(pltpu.make_async_copy(
                ref.at[at:at + TOK, HS:], v_buf.at[d, rows, :HS], sems.at[d, i, 1]))
        return copies

    def arrive(d):
        for i in range(2):
            rows = pl.ds(i * TOK, TOK)
            ref = kv_refs[0]
            pltpu.make_async_copy(ref.at[:, :HS], k_buf.at[d, rows, :], sems.at[d, i, 0]).wait()
            pltpu.make_async_copy(ref.at[:, HS:], v_buf.at[d, rows, :HS], sems.at[d, i, 1]).wait()

    if keep:
        out_ref[:, :keep * HS] = kept_ref[...]

    @pl.when(first >= length)
    def _():
        out_ref[:, keep * HS:] = jnp.zeros((TOK, heads * HS), out_ref.dtype)

    @pl.when(first < length)
    def _():
        q_copies = []
        for h in range(heads):
            at = (base + h) * HS
            q_copies.append(pltpu.make_async_copy(
                q_ref.at[:, at:at + HS], q_buf.at[pl.ds(h * TOK, TOK), :], q_sems.at[h]))
            q_copies[-1].start()
        for d in range(SLOTS):
            @pl.when(d <= z)
            def _():
                for copy in slot_copies(d):
                    copy.start()

        v_buf[:, :, HS:] = jnp.ones((SLOTS, PAIR, HS), jnp.bfloat16)

        def score(t, j):
            return lax.dot_general(
                q_buf[t * ROWS:(t + 1) * ROWS, :], k_buf[j], (((1,), (1,)), ((), ())),
                preferred_element_type=jnp.float32)

        def lane_max(s):
            top = s[:, :HS]
            for i in range(1, PAIR // HS):
                top = jnp.maximum(top, s[:, i * HS:(i + 1) * HS])
            return top

        def score_first(t):
            s = score(t, 0)
            row = lax.broadcasted_iota(jnp.int32, (ROWS, PAIR), 0) & (TOK - 1)
            col = lax.broadcasted_iota(jnp.int32, (ROWS, PAIR), 1)
            seen = (col <= row) | ((col >= TOK) & (x_lo == 1))
            s = jnp.where(seen, s, -1e30)
            s_buf[0] = s
            m_buf[t % 2] = lane_max(s)

        def score_block(t, j):
            s = score(t, j)
            s_buf[j] = s
            m_buf[t % 2] = jnp.maximum(m_buf[t % 2], lane_max(s))

        def finish_max(t):
            m_buf[t % 2] = jnp.broadcast_to(m_buf[t % 2].max(axis=-1, keepdims=True), (ROWS, HS))

        def mix(t, j):
            wide = jnp.concatenate([m_buf[t % 2]] * (PAIR // HS), axis=1)
            p = jnp.exp2((s_buf[j] - wide) * SCALE_LOG2E)
            return jnp.dot(p.astype(jnp.bfloat16), v_buf[j], preferred_element_type=jnp.float32)

        def write_out(t):
            acc = acc_buf[...]
            row = (lax.broadcasted_iota(jnp.int32, (ROWS, HS), 0) & (TOK - 1)) + first
            o = jnp.where(row < length, acc[:, :HS] / acc[:, HS:], 0.0).astype(out_ref.dtype)
            for i in range(ROWS // TOK):
                h = keep + t * (ROWS // TOK) + i
                out_ref[:, h * HS:(h + 1) * HS] = o[i * TOK:(i + 1) * TOK]

        for copy in q_copies:
            copy.wait()
        tiles = heads * TOK // ROWS
        for t in range(tiles + 1):
            if t == 0:
                arrive(0)
            if t > 0:
                acc_buf[...] = mix(t - 1, 0)
            if t < tiles:
                score_first(t)

            def step(j, carry):
                if t == 0:
                    arrive(j)
                if t > 0:
                    acc_buf[...] += mix(t - 1, j)
                if t < tiles:
                    score_block(t, j)
                return carry

            lax.fori_loop(1, z + 1, step, 0)
            if t < tiles:
                finish_max(t)
            if t > 0:
                write_out(t - 1)


def attention(base, heads, info, q, sources, blocks, kept=()):
    keep = base if kept else 0
    width = (keep + heads) * HS
    return pl.pallas_call(
        functools.partial(attention_kernel, base, heads, keep, sources),
        out_shape=jax.ShapeDtypeStruct((TOK, width), jnp.bfloat16),
        in_specs=[SCALARS, ANYWHERE] + [WHOLE] * len(kept) + [ANYWHERE] * len(blocks),
        out_specs=WHOLE,
        scratch_shapes=[
            pltpu.VMEM((heads * TOK, HS), jnp.bfloat16),
            pltpu.VMEM((SLOTS, PAIR, HS), jnp.bfloat16),
            pltpu.VMEM((SLOTS, PAIR, 2 * HS), jnp.bfloat16),
            pltpu.VMEM((SLOTS, ROWS, PAIR), jnp.float32),
            pltpu.VMEM((2, ROWS, HS), jnp.float32),
            pltpu.VMEM((ROWS, 2 * HS), jnp.float32),
            pltpu.SemaphoreType.DMA((SLOTS, 2, 2)),
            pltpu.SemaphoreType.DMA((heads,)),
        ],
        compiler_params=pltpu.CompilerParams(vmem_limit_bytes=VMEM_LIMIT),
        cost_estimate=pl.CostEstimate(flops=heads * 3_500_000_000, bytes_accessed=2 << 20, transcendentals=0),
        name="attention",
    )(info, q, *kept, *blocks)


def projection_kernel(targets, build, info_ref, *rest):
    count = 2 * len(targets)
    inputs = 8 if build else 1
    parts, rest = rest[:inputs], rest[inputs:]
    w_refs, rest = (rest[:SLOTS + 1], rest[SLOTS + 1:2 * SLOTS + 2]), rest[2 * SLOTS + 2:]
    outs, rest = rest[:count], rest[count:]
    if build:
        a_buf, w_buf, sems = rest
    else:
        (a_buf,) = parts
        w_buf, sems = rest
    z = info_ref[0]
    y = info_ref[4]
    x_hi = info_ref[5]
    places = [(r, e) for r in targets for e in range(2)]

    def pair(place, d):
        copies = []
        for side, refs in enumerate(w_refs):
            dst, sem = w_buf.at[place, side], sems.at[place, side]
            if d == 4:
                low = refs[4].shape[0]
                copies.append(pltpu.make_async_copy(refs[4], dst.at[:low, :], sem))
                copies.append(pltpu.make_async_copy(refs[5], dst.at[low:, :], sem))
            else:
                copies.append(pltpu.make_async_copy(refs[d + (d > 4)], dst, sem))
        return copies

    for place, (r, e) in enumerate(places):
        zz = lax.rem(y + r, 4) * 2 + lax.rem(x_hi + e, 2)
        need = lax.rem(z - zz + SLOTS, SLOTS)
        for d in range(SLOTS):
            @pl.when(need == d)
            def _():
                for copy in pair(place, d):
                    copy.start()

    if build:
        att0, near1, near3, att1, mix1, mix3, top, bottom = parts
        half, cut, last = TOK // 2, att0.shape[1], att1.shape[1]
        wide = HEADS * HS
        a_buf[:TOK, :cut] = att0[...]
        a_buf[:TOK, cut:wide] = att1[...]
        a_buf[TOK:, :cut] = near1[...]
        a_buf[TOK:, cut:wide] = mix1[:TOK]
        a_buf[TOK:, wide:wide + cut] = near3[...]
        a_buf[TOK:, wide + cut:] = mix3[:TOK]
        for i in range(cut // last):
            cols = slice(wide + i * last, wide + (i + 1) * last)
            rows = slice(TOK + i * half, TOK + (i + 1) * half)
            a_buf[:half, cols] = mix1[rows]
            a_buf[half:TOK, cols] = mix3[rows]
        a_buf[:half, wide + cut:] = top[...]
        a_buf[half:TOK, wide + cut:] = bottom[...]

    for place, _ in enumerate(places):
        for copy in pair(place, 0):
            copy.wait()
        w = jnp.concatenate([w_buf[place, 0], w_buf[place, 1]], axis=1)
        out = jnp.dot(a_buf[...], w, preferred_element_type=jnp.float32)
        outs[place][...] = out.astype(jnp.bfloat16)


def projection(targets, info, a_parts, weights):
    rows, cols = weights[0].shape
    count = 2 * len(targets)
    build = len(a_parts) > 1
    shapes = [jax.ShapeDtypeStruct((PAIR, 2 * cols), jnp.bfloat16)] * count
    if build:
        shapes.append(jax.ShapeDtypeStruct((PAIR, rows), jnp.bfloat16))
    return pl.pallas_call(
        functools.partial(projection_kernel, targets, build),
        out_shape=shapes,
        in_specs=[SCALARS] + [WHOLE] * len(a_parts) + [ANYWHERE] * len(weights),
        out_specs=[WHOLE] * len(shapes),
        scratch_shapes=[
            pltpu.VMEM((count, 2, rows, cols), jnp.bfloat16),
            pltpu.SemaphoreType.DMA((count, 2)),
        ],
        compiler_params=pltpu.CompilerParams(vmem_limit_bytes=VMEM_LIMIT),
        cost_estimate=pl.CostEstimate(
            flops=count * 800_000_000, bytes_accessed=count << 20, transcendentals=0),
        name="projection",
    )(info, *a_parts, *weights)


def assemble_kernel(info_ref, p0, p1, p2, p3, out_ref):
    x_lo = info_ref[1]
    x_hi = info_ref[5]
    g = info_ref[6]
    for rel, ref in enumerate((p0, p1, p2, p3)):
        src_lo = lax.rem(x_lo + (rel & 1), 2)
        src_hi = lax.rem(x_hi + (rel >> 1), 2)
        base = ((1 - src_lo) * 2 + src_hi) * 256
        for k in range(2):
            at = base + lax.rem(g + k, 2) * HS
            out_ref[:, pl.ds(pl.multiple_of(at, HS), HS)] = ref[:, k * HS:(k + 1) * HS]


def assemble(info, pieces):
    return pl.pallas_call(
        assemble_kernel,
        out_shape=jax.ShapeDtypeStruct((TOK, 4 * pieces[0].shape[1]), jnp.bfloat16),
        in_specs=[SCALARS] + [WHOLE] * 4,
        out_specs=WHOLE,
        compiler_params=pltpu.CompilerParams(vmem_limit_bytes=VMEM_LIMIT),
        name="assemble",
    )(info, *pieces)


def after(value, *others):
    return lax.optimization_barrier((value, *others))[0]


def local(queries, key_rows, value_rows, out_weight, lengths):
    blk = lax.axis_index("blk")
    tp = lax.axis_index("tp")
    g = lax.axis_index("grp")
    z, x_lo = blk // 2, blk % 2
    y, x_hi = tp // 2, tp % 2
    info = jnp.stack([z, x_lo, blk * TOK, lengths[0], y, x_hi, g, jnp.zeros_like(g)]).astype(jnp.int32)

    def z_shift(value, step):
        return lax.ppermute(value, "blk", [(i, (i + 2 * step) % 16) for i in range(16)])

    def y_shift(value, step):
        return lax.ppermute(value, "tp", [(i, (i + 2 * step) % 8) for i in range(8)])

    def x_flip(value, rel):
        if rel == 1:
            return lax.ppermute(value, "blk", [(i, i ^ 1) for i in range(16)])
        if rel == 2:
            return lax.ppermute(value, "tp", [(i, i ^ 1) for i in range(8)])
        return lax.ppermute(value, ("blk", "tp"), [(i, i ^ 9) for i in range(128)])

    def swap(value):
        return lax.ppermute(value, "grp", [(0, 1), (1, 0)])

    quarter = out_weight.shape[1] // 4
    keep_at, give_at = (x_hi * 2 + g) * quarter, ((1 - x_hi) * 2 + g) * quarter
    info, keep_at, give_at = lax.optimization_barrier(
        (info, keep_at.astype(jnp.uint32), give_at.astype(jnp.uint32)))

    own_kv = jnp.concatenate([key_rows[0], value_rows[0]], axis=1)
    own_kv = after(own_kv, info, keep_at, give_at)
    up1, dn1 = z_shift(own_kv, 1), z_shift(own_kv, -1)
    up2, dn2 = z_shift(up1, 1), z_shift(dn1, -1)
    up3, dn3 = z_shift(up2, 1), z_shift(dn2, -1)
    up4 = z_shift(up3, 1)
    blocks = []
    for mine in (own_kv, up1, up2, up3, up4, dn3, dn2, dn1):
        blocks += [mine, x_flip(mine, 1)]
    sources = tuple(((2 * d, 0), (2 * d + 1, 0)) for d in range(SLOTS))

    shape = (out_weight.shape[0], quarter)
    give1 = lax.dynamic_slice(out_weight, (jnp.uint32(0), keep_at), shape)
    give3 = lax.dynamic_slice(out_weight, (jnp.uint32(0), give_at), shape)
    give1, give3 = after(give1, up1), after(give3, up1)
    w0 = jnp.concatenate([x_flip(give1, 1), x_flip(give3, 3)], axis=0)
    w0 = after(w0, dn3)
    rows = w0.shape[0] // 2
    w_up1, w_dn1 = z_shift(w0, 1), z_shift(w0, -1)

    o0 = swap(w0)
    head = after(attention(0, 2, info, queries[0], sources, blocks), o0)
    w_up2, w_dn2 = z_shift(after(w_up1, head), 1), z_shift(after(w_dn1, head), -1)
    o_up1, o_dn1 = swap(w_up1), swap(w_dn1)
    att0 = attention(2, 4, info, queries[0], sources, blocks, (head,))
    att0 = after(att0, o_up1, o_dn1)
    near1, near3 = x_flip(att0, 1), x_flip(att0, 3)
    w_up3, w_dn3 = z_shift(after(w_up2, att0), 1), z_shift(after(w_dn2, att0), -1)
    o_up2, o_dn2 = swap(after(w_up2, att0)), swap(after(w_dn2, att0))
    att1 = attention(6, 2, info, after(queries[0], att0), sources, blocks)
    half, last = TOK // 2, att1.shape[1]

    def message(a, far):
        return jnp.concatenate([a] + [far[:, i:i + last] for i in range(0, far.shape[1], last)], 0)

    send1, send3 = message(att1, near3[:half]), message(att1, near1[half:])
    w_up3, w_dn3, _ = lax.optimization_barrier((w_up3, w_dn3, send3))
    w_up4, w_dn4 = z_shift(w_up3[:rows], 1), z_shift(w_dn3[rows:], -1)
    mix1, mix3, w_up4, w_dn4 = lax.optimization_barrier((x_flip(send1, 1), x_flip(send3, 3), w_up4, w_dn4))
    top, bottom, o_up4, o_dn4 = lax.optimization_barrier(
        (x_flip(mix3[:half], 1), x_flip(mix1[half:TOK], 3), swap(w_up4), swap(w_dn4)))
    a_parts = (att0, near1, near3, att1, mix1, mix3, top, bottom)

    weights = (w0, w_up1, w_up2, w_up3, w_up4, w_dn4, w_dn3, w_dn2, w_dn1,
               o0, o_up1, o_up2, swap(w_up3), o_up4, o_dn4, swap(w_dn3), o_dn2, o_dn1)

    f32 = jnp.float32
    c2s, c2f, a_full = projection((2,), info, a_parts, weights)
    up_2f, dn_2s = y_shift(c2f, 1), y_shift(c2s, -1)
    c1s, c1f, c3s, c3f = projection((1, 3), info, (a_full,), weights)
    up_f = y_shift((c1f.astype(f32) + up_2f.astype(f32)).astype(jnp.bfloat16), 1)
    dn_f = y_shift(c3f, -1)
    sum_s = (c3s.astype(f32) + dn_2s.astype(f32)).astype(jnp.bfloat16)
    up_s, dn_s = y_shift(after(c1s, sum_s), 1), y_shift(sum_s, -1)
    c0s, c0f = projection((0,), info, (a_full,), weights)

    def total(own, up, dn, at):
        rows = slice(at, at + TOK)
        return (own[rows].astype(f32) + up[rows].astype(f32) + dn[rows].astype(f32)).astype(jnp.bfloat16)

    pieces = (
        total(c0s, up_s, dn_s, 0),
        x_flip(total(c0s, up_s, dn_s, TOK), 1),
        x_flip(total(c0f, up_f, dn_f, 0), 2),
        x_flip(total(c0f, up_f, dn_f, TOK), 3),
    )
    return assemble(info, pieces)[None]


def solution(mesh):
    in_specs = (
        P("grp", "blk", "tp"),
        P("grp", "blk", "tp"),
        P("grp", "blk", "tp"),
        P("tp", "blk"),
        P("grp"),
    )
    out_specs = P("grp", "blk", "tp")
    return jax.shard_map(local, mesh=mesh, in_specs=in_specs, out_specs=out_specs, check_vma=False)
```

```python
import functools

import jax
import jax.numpy as jnp
from jax import lax
from jax.experimental import pallas as pl
from jax.experimental.pallas import tpu as pltpu
from jax.sharding import PartitionSpec as P

HS = 128
TOK = 256
HEADS = 8
PAIR = 2 * TOK
SLOTS = 8
ROWS = 512
SCALE_LOG2E = (HS ** -0.5) * 1.4426950408889634
VMEM_LIMIT = 20 * 1024 * 1024
WHOLE = pl.BlockSpec(memory_space=pltpu.VMEM)
ANYWHERE = pl.BlockSpec(memory_space=pl.ANY)
SCALARS = pl.BlockSpec(memory_space=pltpu.SMEM)


def attention_kernel(base, heads, keep, sources, info_ref, q_ref, *rest):
    if keep:
        kept_ref, rest = rest[0], rest[1:]
    kv_count = len(rest) - 9
    kv_refs = rest[:kv_count]
    out_ref, q_buf, k_buf, v_buf, s_buf, m_buf, acc_buf, sems, q_sems = rest[kv_count:]
    z = info_ref[0]
    x_lo = info_ref[1]
    first = info_ref[2]
    length = info_ref[3]

    def slot_copies(d):
        copies = []
        for i, (which, at) in enumerate(sources[d]):
            ref = kv_refs[which]
            rows = pl.ds(i * TOK, TOK)
            copies.append(pltpu.make_async_copy(
                ref.at[at:at + TOK, :HS], k_buf.at[d, rows, :], sems.at[d, i, 0]))
            copies.append(pltpu.make_async_copy(
                ref.at[at:at + TOK, HS:], v_buf.at[d, rows, :HS], sems.at[d, i, 1]))
        return copies

    def arrive(d):
        for i in range(2):
            rows = pl.ds(i * TOK, TOK)
            ref = kv_refs[0]
            pltpu.make_async_copy(ref.at[:, :HS], k_buf.at[d, rows, :], sems.at[d, i, 0]).wait()
            pltpu.make_async_copy(ref.at[:, HS:], v_buf.at[d, rows, :HS], sems.at[d, i, 1]).wait()

    if keep:
        out_ref[:, :keep * HS] = kept_ref[...]

    @pl.when(first >= length)
    def _():
        out_ref[:, keep * HS:] = jnp.zeros((TOK, heads * HS), out_ref.dtype)

    @pl.when(first < length)
    def _():
        q_copies = []
        for h in range(heads):
            at = (base + h) * HS
            q_copies.append(pltpu.make_async_copy(
                q_ref.at[:, at:at + HS], q_buf.at[pl.ds(h * TOK, TOK), :], q_sems.at[h]))
            q_copies[-1].start()
        for d in range(SLOTS):
            @pl.when(d <= z)
            def _():
                for copy in slot_copies(d):
                    copy.start()

        v_buf[:, :, HS:] = jnp.ones((SLOTS, PAIR, HS), jnp.bfloat16)

        def score(t, j, n):
            keys = k_buf[pl.ds(j, n)].reshape(n * PAIR, HS)
            return lax.dot_general(
                q_buf[t * ROWS:(t + 1) * ROWS, :], keys, (((1,), (1,)), ((), ())),
                preferred_element_type=jnp.float32)

        def lane_max(s):
            top = s[:, :HS]
            for i in range(1, s.shape[1] // HS):
                top = jnp.maximum(top, s[:, i * HS:(i + 1) * HS])
            return top

        def score_first(t):
            s = score(t, 0, 1)
            row = lax.broadcasted_iota(jnp.int32, (ROWS, PAIR), 0) & (TOK - 1)
            col = lax.broadcasted_iota(jnp.int32, (ROWS, PAIR), 1)
            seen = (col <= row) | ((col >= TOK) & (x_lo == 1))
            s = jnp.where(seen, s, -1e30)
            s_buf[0] = s
            m_buf[t % 2] = lane_max(s)

        def score_block(t, j, n):
            s = score(t, j, n)
            for i in range(n):
                s_buf[j + i] = s[:, i * PAIR:(i + 1) * PAIR]
            m_buf[t % 2] = jnp.maximum(m_buf[t % 2], lane_max(s))

        def finish_max(t):
            m_buf[t % 2] = jnp.broadcast_to(m_buf[t % 2].max(axis=-1, keepdims=True), (ROWS, HS))

        def mix(t, j, n):
            wide = jnp.concatenate([m_buf[t % 2]] * (PAIR // HS), axis=1)
            p = [jnp.exp2((s_buf[j + i] - wide) * SCALE_LOG2E).astype(jnp.bfloat16) for i in range(n)]
            values = v_buf[pl.ds(j, n)].reshape(n * PAIR, 2 * HS)
            return jnp.dot(jnp.concatenate(p, axis=1), values, preferred_element_type=jnp.float32)

        def write_out(t):
            acc = acc_buf[...]
            row = (lax.broadcasted_iota(jnp.int32, (ROWS, HS), 0) & (TOK - 1)) + first
            o = jnp.where(row < length, acc[:, :HS] / acc[:, HS:], 0.0).astype(out_ref.dtype)
            for i in range(ROWS // TOK):
                h = keep + t * (ROWS // TOK) + i
                out_ref[:, h * HS:(h + 1) * HS] = o[i * TOK:(i + 1) * TOK]

        for copy in q_copies:
            copy.wait()
        tiles = heads * TOK // ROWS
        for t in range(tiles + 1):
            if t == 0:
                arrive(0)
            if t > 0:
                acc_buf[...] = mix(t - 1, 0, 1)
            if t < tiles:
                score_first(t)

            def step(j, n):
                if t == 0:
                    for i in range(n):
                        arrive(j + i)
                if t > 0:
                    acc_buf[...] += mix(t - 1, j, n)
                if t < tiles:
                    score_block(t, j, n)

            def two(i, carry):
                step(1 + 2 * i, 2)
                return carry

            lax.fori_loop(0, z // 2, two, 0)

            @pl.when(z % 2 == 1)
            def _():
                step(z, 1)

            if t < tiles:
                finish_max(t)
            if t > 0:
                write_out(t - 1)


def attention(base, heads, info, q, sources, blocks, kept=()):
    keep = base if kept else 0
    width = (keep + heads) * HS
    return pl.pallas_call(
        functools.partial(attention_kernel, base, heads, keep, sources),
        out_shape=jax.ShapeDtypeStruct((TOK, width), jnp.bfloat16),
        in_specs=[SCALARS, ANYWHERE] + [WHOLE] * len(kept) + [ANYWHERE] * len(blocks),
        out_specs=WHOLE,
        scratch_shapes=[
            pltpu.VMEM((heads * TOK, HS), jnp.bfloat16),
            pltpu.VMEM((SLOTS, PAIR, HS), jnp.bfloat16),
            pltpu.VMEM((SLOTS, PAIR, 2 * HS), jnp.bfloat16),
            pltpu.VMEM((SLOTS, ROWS, PAIR), jnp.float32),
            pltpu.VMEM((2, ROWS, HS), jnp.float32),
            pltpu.VMEM((ROWS, 2 * HS), jnp.float32),
            pltpu.SemaphoreType.DMA((SLOTS, 2, 2)),
            pltpu.SemaphoreType.DMA((heads,)),
        ],
        compiler_params=pltpu.CompilerParams(vmem_limit_bytes=VMEM_LIMIT),
        cost_estimate=pl.CostEstimate(flops=heads * 3_500_000_000, bytes_accessed=2 << 20, transcendentals=0),
        name="attention",
    )(info, q, *kept, *blocks)


def projection_kernel(targets, build, info_ref, *rest):
    count = 2 * len(targets)
    inputs = 8 if build else 1
    parts, rest = rest[:inputs], rest[inputs:]
    w_refs, rest = (rest[:SLOTS + 1], rest[SLOTS + 1:2 * SLOTS + 2]), rest[2 * SLOTS + 2:]
    outs, rest = rest[:count], rest[count:]
    if build:
        a_buf, w_buf, sems = rest
    else:
        (a_buf,) = parts
        w_buf, sems = rest
    z = info_ref[0]
    y = info_ref[4]
    x_hi = info_ref[5]
    places = [(r, e) for r in targets for e in range(2)]

    def pair(place, d):
        copies = []
        for side, refs in enumerate(w_refs):
            dst, sem = w_buf.at[place, side], sems.at[place, side]
            if d == 4:
                low = refs[4].shape[0]
                copies.append(pltpu.make_async_copy(refs[4], dst.at[:low, :], sem))
                copies.append(pltpu.make_async_copy(refs[5], dst.at[low:, :], sem))
            else:
                copies.append(pltpu.make_async_copy(refs[d + (d > 4)], dst, sem))
        return copies

    for place, (r, e) in enumerate(places):
        zz = lax.rem(y + r, 4) * 2 + lax.rem(x_hi + e, 2)
        need = lax.rem(z - zz + SLOTS, SLOTS)
        for d in range(SLOTS):
            @pl.when(need == d)
            def _():
                for copy in pair(place, d):
                    copy.start()

    if build:
        att0, near1, near3, att1, mix1, mix3, top, bottom = parts
        half, cut, last = TOK // 2, att0.shape[1], att1.shape[1]
        wide = HEADS * HS
        a_buf[:TOK, :cut] = att0[...]
        a_buf[:TOK, cut:wide] = att1[...]
        a_buf[TOK:, :cut] = near1[...]
        a_buf[TOK:, cut:wide] = mix1[:TOK]
        a_buf[TOK:, wide:wide + cut] = near3[...]
        a_buf[TOK:, wide + cut:] = mix3[:TOK]
        for i in range(cut // last):
            cols = slice(wide + i * last, wide + (i + 1) * last)
            rows = slice(TOK + i * half, TOK + (i + 1) * half)
            a_buf[:half, cols] = mix1[rows]
            a_buf[half:TOK, cols] = mix3[rows]
        a_buf[:half, wide + cut:] = top[...]
        a_buf[half:TOK, wide + cut:] = bottom[...]

    for place, _ in enumerate(places):
        for copy in pair(place, 0):
            copy.wait()
        w = jnp.concatenate([w_buf[place, 0], w_buf[place, 1]], axis=1)
        out = jnp.dot(a_buf[...], w, preferred_element_type=jnp.float32)
        outs[place][...] = out.astype(jnp.bfloat16)


def projection(targets, info, a_parts, weights):
    rows, cols = weights[0].shape
    count = 2 * len(targets)
    build = len(a_parts) > 1
    shapes = [jax.ShapeDtypeStruct((PAIR, 2 * cols), jnp.bfloat16)] * count
    if build:
        shapes.append(jax.ShapeDtypeStruct((PAIR, rows), jnp.bfloat16))
    return pl.pallas_call(
        functools.partial(projection_kernel, targets, build),
        out_shape=shapes,
        in_specs=[SCALARS] + [WHOLE] * len(a_parts) + [ANYWHERE] * len(weights),
        out_specs=[WHOLE] * len(shapes),
        scratch_shapes=[
            pltpu.VMEM((count, 2, rows, cols), jnp.bfloat16),
            pltpu.SemaphoreType.DMA((count, 2)),
        ],
        compiler_params=pltpu.CompilerParams(vmem_limit_bytes=VMEM_LIMIT),
        cost_estimate=pl.CostEstimate(
            flops=count * 800_000_000, bytes_accessed=count << 20, transcendentals=0),
        name="projection",
    )(info, *a_parts, *weights)


def assemble_kernel(info_ref, p0, p1, p2, p3, out_ref):
    x_lo = info_ref[1]
    x_hi = info_ref[5]
    g = info_ref[6]
    for rel, ref in enumerate((p0, p1, p2, p3)):
        src_lo = lax.rem(x_lo + (rel & 1), 2)
        src_hi = lax.rem(x_hi + (rel >> 1), 2)
        base = ((1 - src_lo) * 2 + src_hi) * 256
        for k in range(2):
            at = base + lax.rem(g + k, 2) * HS
            out_ref[:, pl.ds(pl.multiple_of(at, HS), HS)] = ref[:, k * HS:(k + 1) * HS]


def assemble(info, pieces):
    return pl.pallas_call(
        assemble_kernel,
        out_shape=jax.ShapeDtypeStruct((TOK, 4 * pieces[0].shape[1]), jnp.bfloat16),
        in_specs=[SCALARS] + [WHOLE] * 4,
        out_specs=WHOLE,
        compiler_params=pltpu.CompilerParams(vmem_limit_bytes=VMEM_LIMIT),
        name="assemble",
    )(info, *pieces)


def after(value, *others):
    return lax.optimization_barrier((value, *others))[0]


def local(queries, key_rows, value_rows, out_weight, lengths):
    blk = lax.axis_index("blk")
    tp = lax.axis_index("tp")
    g = lax.axis_index("grp")
    z, x_lo = blk // 2, blk % 2
    y, x_hi = tp // 2, tp % 2
    info = jnp.stack([z, x_lo, blk * TOK, lengths[0], y, x_hi, g, jnp.zeros_like(g)]).astype(jnp.int32)

    def z_shift(value, step):
        return lax.ppermute(value, "blk", [(i, (i + 2 * step) % 16) for i in range(16)])

    def y_shift(value, step):
        return lax.ppermute(value, "tp", [(i, (i + 2 * step) % 8) for i in range(8)])

    def x_flip(value, rel):
        if rel == 1:
            return lax.ppermute(value, "blk", [(i, i ^ 1) for i in range(16)])
        if rel == 2:
            return lax.ppermute(value, "tp", [(i, i ^ 1) for i in range(8)])
        return lax.ppermute(value, ("blk", "tp"), [(i, i ^ 9) for i in range(128)])

    def swap(value):
        return lax.ppermute(value, "grp", [(0, 1), (1, 0)])

    quarter = out_weight.shape[1] // 4
    keep_at, give_at = (x_hi * 2 + g) * quarter, ((1 - x_hi) * 2 + g) * quarter
    info, keep_at, give_at = lax.optimization_barrier(
        (info, keep_at.astype(jnp.uint32), give_at.astype(jnp.uint32)))

    own_kv = jnp.concatenate([key_rows[0], value_rows[0]], axis=1)
    own_kv = after(own_kv, info, keep_at, give_at)
    up1, dn1 = z_shift(own_kv, 1), z_shift(own_kv, -1)
    up2, dn2 = z_shift(up1, 1), z_shift(dn1, -1)
    up3, dn3 = z_shift(up2, 1), z_shift(dn2, -1)
    up4 = z_shift(up3, 1)
    blocks = []
    for mine in (own_kv, up1, up2, up3, up4, dn3, dn2, dn1):
        blocks += [mine, x_flip(mine, 1)]
    sources = tuple(((2 * d, 0), (2 * d + 1, 0)) for d in range(SLOTS))

    shape = (out_weight.shape[0], quarter)
    give1 = lax.dynamic_slice(out_weight, (jnp.uint32(0), keep_at), shape)
    give3 = lax.dynamic_slice(out_weight, (jnp.uint32(0), give_at), shape)
    give1, give3 = after(give1, up1), after(give3, up1)
    w0 = jnp.concatenate([x_flip(give1, 1), x_flip(give3, 3)], axis=0)
    w0 = after(w0, dn3)
    rows = w0.shape[0] // 2
    w_up1, w_dn1 = z_shift(w0, 1), z_shift(w0, -1)

    o0 = swap(w0)
    head = after(attention(0, 2, info, queries[0], sources, blocks), o0)
    w_up2, w_dn2 = z_shift(after(w_up1, head), 1), z_shift(after(w_dn1, head), -1)
    o_up1, o_dn1 = swap(w_up1), swap(w_dn1)
    att0 = attention(2, 4, info, queries[0], sources, blocks, (head,))
    att0 = after(att0, o_up1, o_dn1)
    near1, near3 = x_flip(att0, 1), x_flip(att0, 3)
    w_up3, w_dn3 = z_shift(after(w_up2, att0), 1), z_shift(after(w_dn2, att0), -1)
    o_up2, o_dn2 = swap(after(w_up2, att0)), swap(after(w_dn2, att0))
    att1 = attention(6, 2, info, after(queries[0], att0), sources, blocks)
    half, last = TOK // 2, att1.shape[1]

    def message(a, far):
        return jnp.concatenate([a] + [far[:, i:i + last] for i in range(0, far.shape[1], last)], 0)

    send1, send3 = message(att1, near3[:half]), message(att1, near1[half:])
    w_up3, w_dn3, _ = lax.optimization_barrier((w_up3, w_dn3, send3))
    w_up4, w_dn4 = z_shift(w_up3[:rows], 1), z_shift(w_dn3[rows:], -1)
    mix1, mix3, w_up4, w_dn4 = lax.optimization_barrier((x_flip(send1, 1), x_flip(send3, 3), w_up4, w_dn4))
    top, bottom, o_up4, o_dn4 = lax.optimization_barrier(
        (x_flip(mix3[:half], 1), x_flip(mix1[half:TOK], 3), swap(w_up4), swap(w_dn4)))
    a_parts = (att0, near1, near3, att1, mix1, mix3, top, bottom)

    weights = (w0, w_up1, w_up2, w_up3, w_up4, w_dn4, w_dn3, w_dn2, w_dn1,
               o0, o_up1, o_up2, swap(w_up3), o_up4, o_dn4, swap(w_dn3), o_dn2, o_dn1)

    f32 = jnp.float32
    c2s, c2f, a_full = projection((2,), info, a_parts, weights)
    up_2f, dn_2s = y_shift(c2f, 1), y_shift(c2s, -1)
    c1s, c1f, c3s, c3f = projection((1, 3), info, (a_full,), weights)
    up_f = y_shift((c1f.astype(f32) + up_2f.astype(f32)).astype(jnp.bfloat16), 1)
    dn_f = y_shift(c3f, -1)
    sum_s = (c3s.astype(f32) + dn_2s.astype(f32)).astype(jnp.bfloat16)
    up_s, dn_s = y_shift(after(c1s, sum_s), 1), y_shift(sum_s, -1)
    c0s, c0f = projection((0,), info, (a_full,), weights)

    def total(own, up, dn, at):
        rows = slice(at, at + TOK)
        return (own[rows].astype(f32) + up[rows].astype(f32) + dn[rows].astype(f32)).astype(jnp.bfloat16)

    pieces = (
        total(c0s, up_s, dn_s, 0),
        x_flip(total(c0s, up_s, dn_s, TOK), 1),
        x_flip(total(c0f, up_f, dn_f, 0), 2),
        x_flip(total(c0f, up_f, dn_f, TOK), 3),
    )
    return assemble(info, pieces)[None]


def solution(mesh):
    in_specs = (
        P("grp", "blk", "tp"),
        P("grp", "blk", "tp"),
        P("grp", "blk", "tp"),
        P("tp", "blk"),
        P("grp"),
    )
    out_specs = P("grp", "blk", "tp")
    return jax.shard_map(local, mesh=mesh, in_specs=in_specs, out_specs=out_specs, check_vma=False)
```

```python
import functools

import jax
import jax.numpy as jnp
from jax import lax
from jax.experimental import pallas as pl
from jax.experimental.pallas import tpu as pltpu
from jax.sharding import PartitionSpec as P

HS = 128
TOK = 256
HEADS = 8
PAIR = 2 * TOK
SLOTS = 8
ROWS = 512
SCALE_LOG2E = (HS ** -0.5) * 1.4426950408889634
VMEM_LIMIT = 20 * 1024 * 1024
WHOLE = pl.BlockSpec(memory_space=pltpu.VMEM)
ANYWHERE = pl.BlockSpec(memory_space=pl.ANY)
SCALARS = pl.BlockSpec(memory_space=pltpu.SMEM)


def attention_kernel(base, heads, keep, sources, info_ref, q_ref, *rest):
    if keep:
        kept_ref, rest = rest[0], rest[1:]
    kv_count = len(rest) - 9
    kv_refs = rest[:kv_count]
    out_ref, q_buf, k_buf, v_buf, s_buf, m_buf, acc_buf, sems, q_sems = rest[kv_count:]
    z = info_ref[0]
    x_lo = info_ref[1]
    first = info_ref[2]
    length = info_ref[3]

    def slot_copies(d):
        copies = []
        for i, (which, at) in enumerate(sources[d]):
            ref = kv_refs[which]
            rows = pl.ds(i * TOK, TOK)
            copies.append(pltpu.make_async_copy(
                ref.at[at:at + TOK, :HS], k_buf.at[d, rows, :], sems.at[d, i, 0]))
            copies.append(pltpu.make_async_copy(
                ref.at[at:at + TOK, HS:], v_buf.at[d, rows, :HS], sems.at[d, i, 1]))
        return copies

    def arrive(d):
        for i in range(2):
            rows = pl.ds(i * TOK, TOK)
            ref = kv_refs[0]
            pltpu.make_async_copy(ref.at[:, :HS], k_buf.at[d, rows, :], sems.at[d, i, 0]).wait()
            pltpu.make_async_copy(ref.at[:, HS:], v_buf.at[d, rows, :HS], sems.at[d, i, 1]).wait()

    if keep:
        out_ref[:, :keep * HS] = kept_ref[...]

    @pl.when(first >= length)
    def _():
        out_ref[:, keep * HS:] = jnp.zeros((TOK, heads * HS), out_ref.dtype)

    @pl.when(first < length)
    def _():
        q_copies = []
        for h in range(heads):
            at = (base + h) * HS
            q_copies.append(pltpu.make_async_copy(
                q_ref.at[:, at:at + HS], q_buf.at[pl.ds(h * TOK, TOK), :], q_sems.at[h]))
            q_copies[-1].start()
        for d in range(SLOTS):
            @pl.when(d <= z)
            def _():
                for copy in slot_copies(d):
                    copy.start()

        v_buf[:, :, HS:] = jnp.ones((SLOTS, PAIR, HS), jnp.bfloat16)

        def score(t, j, n):
            keys = k_buf[pl.ds(j, n)].reshape(n * PAIR, HS)
            return lax.dot_general(
                q_buf[t * ROWS:(t + 1) * ROWS, :], keys, (((1,), (1,)), ((), ())),
                preferred_element_type=jnp.float32)

        def lane_max(s):
            top = s[:, :HS]
            for i in range(1, s.shape[1] // HS):
                top = jnp.maximum(top, s[:, i * HS:(i + 1) * HS])
            return top

        def score_first(t):
            s = score(t, 0, 1)
            row = lax.broadcasted_iota(jnp.int32, (ROWS, PAIR), 0) & (TOK - 1)
            col = lax.broadcasted_iota(jnp.int32, (ROWS, PAIR), 1)
            seen = (col <= row) | ((col >= TOK) & (x_lo == 1))
            s = jnp.where(seen, s, -1e30)
            s_buf[0] = s
            m_buf[t % 2] = lane_max(s)

        def score_block(t, j, n):
            s = score(t, j, n)
            for i in range(n):
                s_buf[j + i] = s[:, i * PAIR:(i + 1) * PAIR]
            m_buf[t % 2] = jnp.maximum(m_buf[t % 2], lane_max(s))

        def finish_max(t):
            m_buf[t % 2] = jnp.broadcast_to(m_buf[t % 2].max(axis=-1, keepdims=True), (ROWS, HS))

        def mix(t, j, n):
            wide = jnp.concatenate([m_buf[t % 2]] * (PAIR // HS), axis=1)
            p = [jnp.exp2((s_buf[j + i] - wide) * SCALE_LOG2E).astype(jnp.bfloat16) for i in range(n)]
            values = v_buf[pl.ds(j, n)].reshape(n * PAIR, 2 * HS)
            return jnp.dot(jnp.concatenate(p, axis=1), values, preferred_element_type=jnp.float32)

        def write_out(t):
            acc = acc_buf[...]
            row = (lax.broadcasted_iota(jnp.int32, (ROWS, HS), 0) & (TOK - 1)) + first
            o = jnp.where(row < length, acc[:, :HS] / acc[:, HS:], 0.0).astype(out_ref.dtype)
            for i in range(ROWS // TOK):
                h = keep + t * (ROWS // TOK) + i
                out_ref[:, h * HS:(h + 1) * HS] = o[i * TOK:(i + 1) * TOK]

        for copy in q_copies:
            copy.wait()
        tiles = heads * TOK // ROWS
        for t in range(tiles + 1):
            if t == 0:
                arrive(0)
            if t > 0:
                acc_buf[...] = mix(t - 1, 0, 1)
            if t < tiles:
                score_first(t)

            def step(j, n):
                if t == 0:
                    for i in range(n):
                        arrive(j + i)
                if t > 0:
                    acc_buf[...] += mix(t - 1, j, n)
                if t < tiles:
                    score_block(t, j, n)

            def two(i, carry):
                step(1 + 2 * i, 2)
                return carry

            lax.fori_loop(0, z // 2, two, 0)

            @pl.when(z % 2 == 1)
            def _():
                step(z, 1)

            if t < tiles:
                finish_max(t)
            if t > 0:
                write_out(t - 1)


def attention(base, heads, info, q, sources, blocks, kept=()):
    keep = base if kept else 0
    width = (keep + heads) * HS
    return pl.pallas_call(
        functools.partial(attention_kernel, base, heads, keep, sources),
        out_shape=jax.ShapeDtypeStruct((TOK, width), jnp.bfloat16),
        in_specs=[SCALARS, ANYWHERE] + [WHOLE] * len(kept) + [ANYWHERE] * len(blocks),
        out_specs=WHOLE,
        scratch_shapes=[
            pltpu.VMEM((heads * TOK, HS), jnp.bfloat16),
            pltpu.VMEM((SLOTS, PAIR, HS), jnp.bfloat16),
            pltpu.VMEM((SLOTS, PAIR, 2 * HS), jnp.bfloat16),
            pltpu.VMEM((SLOTS, ROWS, PAIR), jnp.float32),
            pltpu.VMEM((2, ROWS, HS), jnp.float32),
            pltpu.VMEM((ROWS, 2 * HS), jnp.float32),
            pltpu.SemaphoreType.DMA((SLOTS, 2, 2)),
            pltpu.SemaphoreType.DMA((heads,)),
        ],
        compiler_params=pltpu.CompilerParams(vmem_limit_bytes=VMEM_LIMIT),
        cost_estimate=pl.CostEstimate(flops=heads * 3_500_000_000, bytes_accessed=2 << 20, transcendentals=0),
        name="attention",
    )(info, q, *kept, *blocks)


def projection_kernel(places, build, info_ref, *rest):
    count = len(places)
    inputs = 8 if build else 1
    parts, rest = rest[:inputs], rest[inputs:]
    w_refs, rest = (rest[:SLOTS + 1], rest[SLOTS + 1:2 * SLOTS + 2]), rest[2 * SLOTS + 2:]
    outs, rest = rest[:count], rest[count:]
    if build:
        a_buf, w_buf, sems = rest
    else:
        (a_buf,) = parts
        w_buf, sems = rest
    z = info_ref[0]
    y = info_ref[4]
    x_hi = info_ref[5]

    def pair(place, d):
        copies = []
        for side, refs in enumerate(w_refs):
            dst, sem = w_buf.at[place, side], sems.at[place, side]
            if d == 4:
                low = refs[4].shape[0]
                copies.append(pltpu.make_async_copy(refs[4], dst.at[:low, :], sem))
                copies.append(pltpu.make_async_copy(refs[5], dst.at[low:, :], sem))
            else:
                copies.append(pltpu.make_async_copy(refs[d + (d > 4)], dst, sem))
        return copies

    for place, (r, e) in enumerate(places):
        zz = lax.rem(y + r, 4) * 2 + lax.rem(x_hi + e, 2)
        need = lax.rem(z - zz + SLOTS, SLOTS)
        for d in range(SLOTS):
            @pl.when(need == d)
            def _():
                for copy in pair(place, d):
                    copy.start()

    if build:
        att0, near1, near3, att1, mix1, mix3, top, bottom = parts
        half, cut, last = TOK // 2, att0.shape[1], att1.shape[1]
        wide = HEADS * HS
        a_buf[:TOK, :cut] = att0[...]
        a_buf[:TOK, cut:wide] = att1[...]
        a_buf[TOK:, :cut] = near1[...]
        a_buf[TOK:, cut:wide] = mix1[:TOK]
        a_buf[TOK:, wide:wide + cut] = near3[...]
        a_buf[TOK:, wide + cut:] = mix3[:TOK]
        for i in range(cut // last):
            cols = slice(wide + i * last, wide + (i + 1) * last)
            rows = slice(TOK + i * half, TOK + (i + 1) * half)
            a_buf[:half, cols] = mix1[rows]
            a_buf[half:TOK, cols] = mix3[rows]
        a_buf[:half, wide + cut:] = top[...]
        a_buf[half:TOK, wide + cut:] = bottom[...]

    for place, _ in enumerate(places):
        for copy in pair(place, 0):
            copy.wait()
        w = jnp.concatenate([w_buf[place, 0], w_buf[place, 1]], axis=1)
        out = jnp.dot(a_buf[...], w, preferred_element_type=jnp.float32)
        outs[place][...] = out.astype(jnp.bfloat16)


def projection(places, info, a_parts, weights):
    rows, cols = weights[0].shape
    count = len(places)
    build = len(a_parts) > 1
    shapes = [jax.ShapeDtypeStruct((PAIR, 2 * cols), jnp.bfloat16)] * count
    if build:
        shapes.append(jax.ShapeDtypeStruct((PAIR, rows), jnp.bfloat16))
    return pl.pallas_call(
        functools.partial(projection_kernel, places, build),
        out_shape=shapes,
        in_specs=[SCALARS] + [WHOLE] * len(a_parts) + [ANYWHERE] * len(weights),
        out_specs=[WHOLE] * len(shapes),
        scratch_shapes=[
            pltpu.VMEM((count, 2, rows, cols), jnp.bfloat16),
            pltpu.SemaphoreType.DMA((count, 2)),
        ],
        compiler_params=pltpu.CompilerParams(vmem_limit_bytes=VMEM_LIMIT),
        cost_estimate=pl.CostEstimate(
            flops=count * 800_000_000, bytes_accessed=count << 20, transcendentals=0),
        name="projection",
    )(info, *a_parts, *weights)


def assemble_kernel(info_ref, p0, p1, p2, p3, out_ref):
    x_lo = info_ref[1]
    x_hi = info_ref[5]
    g = info_ref[6]
    for rel, ref in enumerate((p0, p1, p2, p3)):
        src_lo = lax.rem(x_lo + (rel & 1), 2)
        src_hi = lax.rem(x_hi + (rel >> 1), 2)
        base = ((1 - src_lo) * 2 + src_hi) * 256
        for k in range(2):
            at = base + lax.rem(g + k, 2) * HS
            out_ref[:, pl.ds(pl.multiple_of(at, HS), HS)] = ref[:, k * HS:(k + 1) * HS]


def assemble(info, pieces):
    return pl.pallas_call(
        assemble_kernel,
        out_shape=jax.ShapeDtypeStruct((TOK, 4 * pieces[0].shape[1]), jnp.bfloat16),
        in_specs=[SCALARS] + [WHOLE] * 4,
        out_specs=WHOLE,
        compiler_params=pltpu.CompilerParams(vmem_limit_bytes=VMEM_LIMIT),
        name="assemble",
    )(info, *pieces)


def after(value, *others):
    return lax.optimization_barrier((value, *others))[0]


def local(queries, key_rows, value_rows, out_weight, lengths):
    blk = lax.axis_index("blk")
    tp = lax.axis_index("tp")
    g = lax.axis_index("grp")
    z, x_lo = blk // 2, blk % 2
    y, x_hi = tp // 2, tp % 2
    info = jnp.stack([z, x_lo, blk * TOK, lengths[0], y, x_hi, g, jnp.zeros_like(g)]).astype(jnp.int32)

    def z_shift(value, step):
        return lax.ppermute(value, "blk", [(i, (i + 2 * step) % 16) for i in range(16)])

    def y_shift(value, step):
        return lax.ppermute(value, "tp", [(i, (i + 2 * step) % 8) for i in range(8)])

    def x_flip(value, rel):
        if rel == 1:
            return lax.ppermute(value, "blk", [(i, i ^ 1) for i in range(16)])
        if rel == 2:
            return lax.ppermute(value, "tp", [(i, i ^ 1) for i in range(8)])
        return lax.ppermute(value, ("blk", "tp"), [(i, i ^ 9) for i in range(128)])

    def swap(value):
        return lax.ppermute(value, "grp", [(0, 1), (1, 0)])

    quarter = out_weight.shape[1] // 4
    keep_at, give_at = (x_hi * 2 + g) * quarter, ((1 - x_hi) * 2 + g) * quarter
    info, keep_at, give_at = lax.optimization_barrier(
        (info, keep_at.astype(jnp.uint32), give_at.astype(jnp.uint32)))

    own_kv = jnp.concatenate([key_rows[0], value_rows[0]], axis=1)
    own_kv = after(own_kv, info, keep_at, give_at)
    up1, dn1 = z_shift(own_kv, 1), z_shift(own_kv, -1)
    up2, dn2 = z_shift(up1, 1), z_shift(dn1, -1)
    up3, dn3 = z_shift(up2, 1), z_shift(dn2, -1)
    up4 = z_shift(up3, 1)
    blocks = []
    for mine in (own_kv, up1, up2, up3, up4, dn3, dn2, dn1):
        blocks += [mine, x_flip(mine, 1)]
    sources = tuple(((2 * d, 0), (2 * d + 1, 0)) for d in range(SLOTS))

    shape = (out_weight.shape[0], quarter)
    give1 = lax.dynamic_slice(out_weight, (jnp.uint32(0), keep_at), shape)
    give3 = lax.dynamic_slice(out_weight, (jnp.uint32(0), give_at), shape)
    give1, give3 = after(give1, up1), after(give3, up1)
    w0 = jnp.concatenate([x_flip(give1, 1), x_flip(give3, 3)], axis=0)
    w0 = after(w0, dn3)
    rows = w0.shape[0] // 2
    w_up1, w_dn1 = z_shift(w0, 1), z_shift(w0, -1)

    o0 = swap(w0)
    head = after(attention(0, 2, info, queries[0], sources, blocks), o0)
    w_up2, w_dn2 = z_shift(after(w_up1, head), 1), z_shift(after(w_dn1, head), -1)
    o_up1, o_dn1 = swap(w_up1), swap(w_dn1)
    att0 = attention(2, 4, info, queries[0], sources, blocks, (head,))
    att0 = after(att0, o_up1, o_dn1)
    near1, near3 = x_flip(att0, 1), x_flip(att0, 3)
    w_up3, w_dn3 = z_shift(after(w_up2, att0), 1), z_shift(after(w_dn2, att0), -1)
    o_up2, o_dn2 = swap(after(w_up2, att0)), swap(after(w_dn2, att0))
    att1 = attention(6, 2, info, after(queries[0], att0), sources, blocks)
    half, last = TOK // 2, att1.shape[1]

    def message(a, far):
        return jnp.concatenate([a] + [far[:, i:i + last] for i in range(0, far.shape[1], last)], 0)

    send1, send3 = message(att1, near3[:half]), message(att1, near1[half:])
    w_up3, w_dn3, _ = lax.optimization_barrier((w_up3, w_dn3, send3))
    w_up4, w_dn4 = z_shift(w_up3[:rows], 1), z_shift(w_dn3[rows:], -1)
    mix1, mix3, w_up4, w_dn4 = lax.optimization_barrier((x_flip(send1, 1), x_flip(send3, 3), w_up4, w_dn4))
    top, bottom, o_up4, o_dn4 = lax.optimization_barrier(
        (x_flip(mix3[:half], 1), x_flip(mix1[half:TOK], 3), swap(w_up4), swap(w_dn4)))
    a_parts = (att0, near1, near3, att1, mix1, mix3, top, bottom)

    weights = (w0, w_up1, w_up2, w_up3, w_up4, w_dn4, w_dn3, w_dn2, w_dn1,
               o0, o_up1, o_up2, swap(w_up3), o_up4, o_dn4, swap(w_dn3), o_dn2, o_dn1)

    f32 = jnp.float32
    c2s, c2f, a_full = projection(((2, 0), (2, 1)), info, a_parts, weights)
    up_2f, dn_2s = lax.optimization_barrier((y_shift(c2f, 1), y_shift(c2s, -1)))
    c1s, c3f = projection(((1, 0), (3, 1)), info, (a_full,), weights)
    up_s, dn_f = lax.optimization_barrier((y_shift(c1s, 1), y_shift(c3f, -1)))
    c1f, c3s = projection(((1, 1), (3, 0)), info, (after(a_full, c1s),), weights)
    sum_f = (c1f.astype(f32) + up_2f.astype(f32)).astype(jnp.bfloat16)
    sum_s = (c3s.astype(f32) + dn_2s.astype(f32)).astype(jnp.bfloat16)
    up_f, dn_s = y_shift(after(sum_f, up_s, dn_f), 1), y_shift(after(sum_s, up_s, dn_f), -1)
    c0s, c0f = projection(((0, 0), (0, 1)), info, (after(a_full, sum_f, sum_s),), weights)

    def total(own, up, dn, at):
        rows = slice(at, at + TOK)
        return (own[rows].astype(f32) + up[rows].astype(f32) + dn[rows].astype(f32)).astype(jnp.bfloat16)

    pieces = (
        total(c0s, up_s, dn_s, 0),
        x_flip(total(c0s, up_s, dn_s, TOK), 1),
        x_flip(total(c0f, up_f, dn_f, 0), 2),
        x_flip(total(c0f, up_f, dn_f, TOK), 3),
    )
    return assemble(info, pieces)[None]


def solution(mesh):
    in_specs = (
        P("grp", "blk", "tp"),
        P("grp", "blk", "tp"),
        P("grp", "blk", "tp"),
        P("tp", "blk"),
        P("grp"),
    )
    out_specs = P("grp", "blk", "tp")
    return jax.shard_map(local, mesh=mesh, in_specs=in_specs, out_specs=out_specs, check_vma=False)
```

```python
import functools

import jax
import jax.numpy as jnp
from jax import lax
from jax.experimental import pallas as pl
from jax.experimental.pallas import tpu as pltpu
from jax.sharding import PartitionSpec as P

HS = 128
TOK = 256
HEADS = 8
PAIR = 2 * TOK
SLOTS = 8
ROWS = 512
SCALE_LOG2E = (HS ** -0.5) * 1.4426950408889634
VMEM_LIMIT = 20 * 1024 * 1024
WHOLE = pl.BlockSpec(memory_space=pltpu.VMEM)
ANYWHERE = pl.BlockSpec(memory_space=pl.ANY)
SCALARS = pl.BlockSpec(memory_space=pltpu.SMEM)


def attention_kernel(base, heads, keep, sources, info_ref, q_ref, *rest):
    if keep:
        kept_ref, rest = rest[0], rest[1:]
    kv_count = len(rest) - 9
    kv_refs = rest[:kv_count]
    out_ref, q_buf, k_buf, v_buf, s_buf, m_buf, acc_buf, sems, q_sems = rest[kv_count:]
    z = info_ref[0]
    x_lo = info_ref[1]
    first = info_ref[2]
    length = info_ref[3]

    def slot_copies(d):
        copies = []
        for i, (which, at) in enumerate(sources[d]):
            ref = kv_refs[which]
            rows = pl.ds(i * TOK, TOK)
            copies.append(pltpu.make_async_copy(
                ref.at[at:at + TOK, :HS], k_buf.at[d, rows, :], sems.at[d, i, 0]))
            copies.append(pltpu.make_async_copy(
                ref.at[at:at + TOK, HS:], v_buf.at[d, rows, :HS], sems.at[d, i, 1]))
        return copies

    def arrive(d):
        for i in range(2):
            rows = pl.ds(i * TOK, TOK)
            ref = kv_refs[0]
            pltpu.make_async_copy(ref.at[:, :HS], k_buf.at[d, rows, :], sems.at[d, i, 0]).wait()
            pltpu.make_async_copy(ref.at[:, HS:], v_buf.at[d, rows, :HS], sems.at[d, i, 1]).wait()

    if keep:
        out_ref[:, :keep * HS] = kept_ref[...]

    @pl.when(first >= length)
    def _():
        out_ref[:, keep * HS:] = jnp.zeros((TOK, heads * HS), out_ref.dtype)

    @pl.when(first < length)
    def _():
        q_copies = []
        for h in range(heads):
            at = (base + h) * HS
            q_copies.append(pltpu.make_async_copy(
                q_ref.at[:, at:at + HS], q_buf.at[pl.ds(h * TOK, TOK), :], q_sems.at[h]))
            q_copies[-1].start()
        for d in range(SLOTS):
            @pl.when(d <= z)
            def _():
                for copy in slot_copies(d):
                    copy.start()

        v_buf[:, :, HS:] = jnp.ones((SLOTS, PAIR, HS), jnp.bfloat16)

        def score(t, j, n):
            keys = k_buf[pl.ds(j, n)].reshape(n * PAIR, HS)
            return lax.dot_general(
                q_buf[t * ROWS:(t + 1) * ROWS, :], keys, (((1,), (1,)), ((), ())),
                preferred_element_type=jnp.float32)

        def lane_max(s):
            top = s[:, :HS]
            for i in range(1, s.shape[1] // HS):
                top = jnp.maximum(top, s[:, i * HS:(i + 1) * HS])
            return top

        def score_first(t):
            s = score(t, 0, 1)
            row = lax.broadcasted_iota(jnp.int32, (ROWS, PAIR), 0) & (TOK - 1)
            col = lax.broadcasted_iota(jnp.int32, (ROWS, PAIR), 1)
            seen = (col <= row) | ((col >= TOK) & (x_lo == 1))
            s = jnp.where(seen, s, -1e30)
            s_buf[0] = s
            m_buf[t % 2] = lane_max(s)

        def score_block(t, j, n):
            s = score(t, j, n)
            for i in range(n):
                s_buf[j + i] = s[:, i * PAIR:(i + 1) * PAIR]
            m_buf[t % 2] = jnp.maximum(m_buf[t % 2], lane_max(s))

        def finish_max(t):
            m_buf[t % 2] = jnp.broadcast_to(m_buf[t % 2].max(axis=-1, keepdims=True), (ROWS, HS))

        def mix(t, j, n):
            wide = jnp.concatenate([m_buf[t % 2]] * (PAIR // HS), axis=1)
            p = [jnp.exp2((s_buf[j + i] - wide) * SCALE_LOG2E).astype(jnp.bfloat16) for i in range(n)]
            values = v_buf[pl.ds(j, n)].reshape(n * PAIR, 2 * HS)
            return jnp.dot(jnp.concatenate(p, axis=1), values, preferred_element_type=jnp.float32)

        def write_out(t):
            acc = acc_buf[...]
            row = (lax.broadcasted_iota(jnp.int32, (ROWS, HS), 0) & (TOK - 1)) + first
            o = jnp.where(row < length, acc[:, :HS] / acc[:, HS:], 0.0).astype(out_ref.dtype)
            for i in range(ROWS // TOK):
                h = keep + t * (ROWS // TOK) + i
                out_ref[:, h * HS:(h + 1) * HS] = o[i * TOK:(i + 1) * TOK]

        for copy in q_copies:
            copy.wait()
        tiles = heads * TOK // ROWS
        for t in range(tiles + 1):
            if t == 0:
                arrive(0)
            if t > 0:
                acc_buf[...] = mix(t - 1, 0, 1)
            if t < tiles:
                score_first(t)

            def step(j, n):
                if t == 0:
                    for i in range(n):
                        arrive(j + i)
                if t > 0:
                    acc_buf[...] += mix(t - 1, j, n)
                if t < tiles:
                    score_block(t, j, n)

            def two(i, carry):
                step(1 + 2 * i, 2)
                return carry

            lax.fori_loop(0, z // 2, two, 0)

            @pl.when(z % 2 == 1)
            def _():
                step(z, 1)

            if t < tiles:
                finish_max(t)
            if t > 0:
                write_out(t - 1)


def attention(base, heads, info, q, sources, blocks, kept=()):
    keep = base if kept else 0
    width = (keep + heads) * HS
    return pl.pallas_call(
        functools.partial(attention_kernel, base, heads, keep, sources),
        out_shape=jax.ShapeDtypeStruct((TOK, width), jnp.bfloat16),
        in_specs=[SCALARS, ANYWHERE] + [WHOLE] * len(kept) + [ANYWHERE] * len(blocks),
        out_specs=WHOLE,
        scratch_shapes=[
            pltpu.VMEM((heads * TOK, HS), jnp.bfloat16),
            pltpu.VMEM((SLOTS, PAIR, HS), jnp.bfloat16),
            pltpu.VMEM((SLOTS, PAIR, 2 * HS), jnp.bfloat16),
            pltpu.VMEM((SLOTS, ROWS, PAIR), jnp.float32),
            pltpu.VMEM((2, ROWS, HS), jnp.float32),
            pltpu.VMEM((ROWS, 2 * HS), jnp.float32),
            pltpu.SemaphoreType.DMA((SLOTS, 2, 2)),
            pltpu.SemaphoreType.DMA((heads,)),
        ],
        compiler_params=pltpu.CompilerParams(vmem_limit_bytes=VMEM_LIMIT),
        cost_estimate=pl.CostEstimate(flops=heads * 3_500_000_000, bytes_accessed=2 << 20, transcendentals=0),
        name="attention",
    )(info, q, *kept, *blocks)


def projection_kernel(places, build, info_ref, *rest):
    count = len(places)
    inputs = 7 if build else 1
    parts, rest = rest[:inputs], rest[inputs:]
    w_refs, rest = (rest[:SLOTS + 1], rest[SLOTS + 1:2 * SLOTS + 2]), rest[2 * SLOTS + 2:]
    outs, rest = rest[:count], rest[count:]
    if build:
        a_buf, w_buf, sems = rest
    else:
        (a_buf,) = parts
        w_buf, sems = rest
    z = info_ref[0]
    y = info_ref[4]
    x_hi = info_ref[5]

    def pair(place, d):
        copies = []
        for side, refs in enumerate(w_refs):
            dst, sem = w_buf.at[place, side], sems.at[place, side]
            if d == 4:
                low = refs[4].shape[0]
                copies.append(pltpu.make_async_copy(refs[4], dst.at[:low, :], sem))
                copies.append(pltpu.make_async_copy(refs[5], dst.at[low:, :], sem))
            else:
                copies.append(pltpu.make_async_copy(refs[d + (d > 4)], dst, sem))
        return copies

    for place, (r, e) in enumerate(places):
        zz = lax.rem(y + r, 4) * 2 + lax.rem(x_hi + e, 2)
        need = lax.rem(z - zz + SLOTS, SLOTS)
        for d in range(SLOTS):
            @pl.when(need == d)
            def _():
                for copy in pair(place, d):
                    copy.start()

    if build:
        att0, near1, near3, att1, mix1, mix3, far = parts
        half, cut, last = TOK // 2, att0.shape[1], att1.shape[1]
        wide = HEADS * HS
        a_buf[:TOK, :cut] = att0[...]
        a_buf[:TOK, cut:wide] = att1[...]
        a_buf[TOK:, :cut] = near1[...]
        a_buf[TOK:, cut:wide] = mix1[:TOK]
        a_buf[TOK:, wide:wide + cut] = near3[...]
        a_buf[TOK:, wide + cut:] = mix3[:TOK]
        for i in range(cut // last):
            cols = slice(wide + i * last, wide + (i + 1) * last)
            rows = slice(TOK + i * half, TOK + (i + 1) * half)
            a_buf[:half, cols] = mix1[rows]
            a_buf[half:TOK, cols] = mix3[rows]
        a_buf[:TOK, wide + cut:] = far[...]

    for place, _ in enumerate(places):
        for copy in pair(place, 0):
            copy.wait()
        w = jnp.concatenate([w_buf[place, 0], w_buf[place, 1]], axis=1)
        out = jnp.dot(a_buf[...], w, preferred_element_type=jnp.float32)
        outs[place][...] = out.astype(jnp.bfloat16)


def projection(places, info, a_parts, weights):
    rows, cols = weights[0].shape
    count = len(places)
    build = len(a_parts) > 1
    shapes = [jax.ShapeDtypeStruct((PAIR, 2 * cols), jnp.bfloat16)] * count
    if build:
        shapes.append(jax.ShapeDtypeStruct((PAIR, rows), jnp.bfloat16))
    return pl.pallas_call(
        functools.partial(projection_kernel, places, build),
        out_shape=shapes,
        in_specs=[SCALARS] + [WHOLE] * len(a_parts) + [ANYWHERE] * len(weights),
        out_specs=[WHOLE] * len(shapes),
        scratch_shapes=[
            pltpu.VMEM((count, 2, rows, cols), jnp.bfloat16),
            pltpu.SemaphoreType.DMA((count, 2)),
        ],
        compiler_params=pltpu.CompilerParams(vmem_limit_bytes=VMEM_LIMIT),
        cost_estimate=pl.CostEstimate(
            flops=count * 800_000_000, bytes_accessed=count << 20, transcendentals=0),
        name="projection",
    )(info, *a_parts, *weights)


def assemble_kernel(info_ref, p0, p1, p2, p3, out_ref):
    x_lo = info_ref[1]
    x_hi = info_ref[5]
    g = info_ref[6]
    for rel, ref in enumerate((p0, p1, p2, p3)):
        src_lo = lax.rem(x_lo + (rel & 1), 2)
        src_hi = lax.rem(x_hi + (rel >> 1), 2)
        base = ((1 - src_lo) * 2 + src_hi) * 256
        for k in range(2):
            at = base + lax.rem(g + k, 2) * HS
            out_ref[:, pl.ds(pl.multiple_of(at, HS), HS)] = ref[:, k * HS:(k + 1) * HS]


def assemble(info, pieces):
    return pl.pallas_call(
        assemble_kernel,
        out_shape=jax.ShapeDtypeStruct((TOK, 4 * pieces[0].shape[1]), jnp.bfloat16),
        in_specs=[SCALARS] + [WHOLE] * 4,
        out_specs=WHOLE,
        compiler_params=pltpu.CompilerParams(vmem_limit_bytes=VMEM_LIMIT),
        name="assemble",
    )(info, *pieces)


def after(value, *others):
    return lax.optimization_barrier((value, *others))[0]


def local(queries, key_rows, value_rows, out_weight, lengths):
    blk = lax.axis_index("blk")
    tp = lax.axis_index("tp")
    g = lax.axis_index("grp")
    z, x_lo = blk // 2, blk % 2
    y, x_hi = tp // 2, tp % 2
    info = jnp.stack([z, x_lo, blk * TOK, lengths[0], y, x_hi, g, jnp.zeros_like(g)]).astype(jnp.int32)

    def z_shift(value, step):
        return lax.ppermute(value, "blk", [(i, (i + 2 * step) % 16) for i in range(16)])

    def y_shift(value, step):
        return lax.ppermute(value, "tp", [(i, (i + 2 * step) % 8) for i in range(8)])

    def x_flip(value, rel):
        if rel == 1:
            return lax.ppermute(value, "blk", [(i, i ^ 1) for i in range(16)])
        if rel == 2:
            return lax.ppermute(value, "tp", [(i, i ^ 1) for i in range(8)])
        return lax.ppermute(value, ("blk", "tp"), [(i, i ^ 9) for i in range(128)])

    def swap(value):
        return lax.ppermute(value, "grp", [(0, 1), (1, 0)])

    quarter = out_weight.shape[1] // 4
    keep_at, give_at = (x_hi * 2 + g) * quarter, ((1 - x_hi) * 2 + g) * quarter
    info, keep_at, give_at = lax.optimization_barrier(
        (info, keep_at.astype(jnp.uint32), give_at.astype(jnp.uint32)))

    own_kv = jnp.concatenate([key_rows[0], value_rows[0]], axis=1)
    own_kv = after(own_kv, info, keep_at, give_at)
    up1, dn1 = z_shift(own_kv, 1), z_shift(own_kv, -1)
    up2, dn2 = z_shift(up1, 1), z_shift(dn1, -1)
    up3, dn3 = z_shift(up2, 1), z_shift(dn2, -1)
    up4 = z_shift(up3, 1)
    blocks = []
    for mine in (own_kv, up1, up2, up3, up4, dn3, dn2, dn1):
        blocks += [mine, x_flip(mine, 1)]
    sources = tuple(((2 * d, 0), (2 * d + 1, 0)) for d in range(SLOTS))

    shape = (out_weight.shape[0], quarter)
    give1 = lax.dynamic_slice(out_weight, (jnp.uint32(0), keep_at), shape)
    give3 = lax.dynamic_slice(out_weight, (jnp.uint32(0), give_at), shape)
    give1, give3 = after(give1, up1), after(give3, up1)
    w0 = jnp.concatenate([x_flip(give1, 1), x_flip(give3, 3)], axis=0)
    w0 = after(w0, dn3)
    rows = w0.shape[0] // 2
    w_up1, w_dn1 = z_shift(w0, 1), z_shift(w0, -1)

    o0 = swap(w0)
    head = after(attention(0, 2, info, queries[0], sources, blocks), o0)
    w_up2, w_dn2 = z_shift(after(w_up1, head), 1), z_shift(after(w_dn1, head), -1)
    o_up1, o_dn1 = swap(w_up1), swap(w_dn1)
    att0 = attention(2, 4, info, queries[0], sources, blocks, (head,))
    att0 = after(att0, o_up1, o_dn1)
    near1, near3 = x_flip(att0, 1), x_flip(att0, 3)
    w_up3, w_dn3 = z_shift(after(w_up2, att0), 1), z_shift(after(w_dn2, att0), -1)
    o_up2, o_dn2 = swap(after(w_up2, att0)), swap(after(w_dn2, att0))
    att1 = attention(6, 2, info, after(queries[0], att0), sources, blocks)
    half, last = TOK // 2, att1.shape[1]

    def message(a, far):
        return jnp.concatenate([a] + [far[:, i:i + last] for i in range(0, far.shape[1], last)], 0)

    send1, send3 = message(att1, near3[:half]), message(att1, near1[half:])
    w_up3, w_dn3, _ = lax.optimization_barrier((w_up3, w_dn3, send3))
    w_up4, w_dn4 = z_shift(w_up3[:rows], 1), z_shift(w_dn3[rows:], -1)
    mix1, mix3, w_up4, w_dn4 = lax.optimization_barrier((x_flip(send1, 1), x_flip(send3, 3), w_up4, w_dn4))
    far, o_up4, o_dn4 = lax.optimization_barrier(
        (x_flip(after(att1, mix1), 2), swap(w_up4), swap(w_dn4)))
    a_parts = (att0, near1, near3, att1, mix1, mix3, far)

    weights = (w0, w_up1, w_up2, w_up3, w_up4, w_dn4, w_dn3, w_dn2, w_dn1,
               o0, o_up1, o_up2, swap(w_up3), o_up4, o_dn4, swap(w_dn3), o_dn2, o_dn1)

    f32 = jnp.float32
    c2s, c2f, a_full = projection(((2, 0), (2, 1)), info, a_parts, weights)
    up_2f, dn_2s = lax.optimization_barrier((y_shift(c2f, 1), y_shift(c2s, -1)))
    c1s, c3f = projection(((1, 0), (3, 1)), info, (a_full,), weights)
    up_s, dn_f = lax.optimization_barrier((y_shift(c1s, 1), y_shift(c3f, -1)))
    c1f, c3s = projection(((1, 1), (3, 0)), info, (after(a_full, c1s),), weights)
    sum_f = (c1f.astype(f32) + up_2f.astype(f32)).astype(jnp.bfloat16)
    sum_s = (c3s.astype(f32) + dn_2s.astype(f32)).astype(jnp.bfloat16)
    sum_f, sum_s = lax.optimization_barrier((sum_f, sum_s))
    up_f, dn_s = lax.optimization_barrier((y_shift(sum_f, 1), y_shift(sum_s, -1)))
    c0s, c0f = projection(((0, 0), (0, 1)), info, (after(a_full, sum_f, sum_s, up_s, dn_f),), weights)

    def total(own, up, dn, at):
        rows = slice(at, at + TOK)
        return (own[rows].astype(f32) + up[rows].astype(f32) + dn[rows].astype(f32)).astype(jnp.bfloat16)

    pieces = (
        total(c0s, up_s, dn_s, 0),
        x_flip(total(c0s, up_s, dn_s, TOK), 1),
        x_flip(total(c0f, up_f, dn_f, 0), 2),
        x_flip(total(c0f, up_f, dn_f, TOK), 3),
    )
    return assemble(info, pieces)[None]


def solution(mesh):
    in_specs = (
        P("grp", "blk", "tp"),
        P("grp", "blk", "tp"),
        P("grp", "blk", "tp"),
        P("tp", "blk"),
        P("grp"),
    )
    out_specs = P("grp", "blk", "tp")
    return jax.shard_map(local, mesh=mesh, in_specs=in_specs, out_specs=out_specs, check_vma=False)
```

```python
import functools

import jax
import jax.numpy as jnp
from jax import lax
from jax.experimental import pallas as pl
from jax.experimental.pallas import tpu as pltpu
from jax.sharding import PartitionSpec as P

HS = 128
TOK = 256
HEADS = 8
PAIR = 2 * TOK
SLOTS = 8
ROWS = 512
SCALE_LOG2E = (HS ** -0.5) * 1.4426950408889634
VMEM_LIMIT = 20 * 1024 * 1024
WHOLE = pl.BlockSpec(memory_space=pltpu.VMEM)
ANYWHERE = pl.BlockSpec(memory_space=pl.ANY)
SCALARS = pl.BlockSpec(memory_space=pltpu.SMEM)


def attention_kernel(base, heads, keep, sources, info_ref, q_ref, *rest):
    if keep:
        kept_ref, rest = rest[0], rest[1:]
    kv_count = len(rest) - 9
    kv_refs = rest[:kv_count]
    out_ref, q_buf, k_buf, v_buf, s_buf, m_buf, acc_buf, sems, q_sems = rest[kv_count:]
    z = info_ref[0]
    x_lo = info_ref[1]
    first = info_ref[2]
    length = info_ref[3]

    def slot_copies(d):
        copies = []
        for i, (which, at) in enumerate(sources[d]):
            ref = kv_refs[which]
            rows = pl.ds(i * TOK, TOK)
            copies.append(pltpu.make_async_copy(
                ref.at[at:at + TOK, :HS], k_buf.at[d, rows, :], sems.at[d, i, 0]))
            copies.append(pltpu.make_async_copy(
                ref.at[at:at + TOK, HS:], v_buf.at[d, rows, :HS], sems.at[d, i, 1]))
        return copies

    def arrive(d):
        for i in range(2):
            rows = pl.ds(i * TOK, TOK)
            ref = kv_refs[0]
            pltpu.make_async_copy(ref.at[:, :HS], k_buf.at[d, rows, :], sems.at[d, i, 0]).wait()
            pltpu.make_async_copy(ref.at[:, HS:], v_buf.at[d, rows, :HS], sems.at[d, i, 1]).wait()

    if keep:
        out_ref[:, :keep * HS] = kept_ref[...]

    @pl.when(first >= length)
    def _():
        out_ref[:, keep * HS:] = jnp.zeros((TOK, heads * HS), out_ref.dtype)

    @pl.when(first < length)
    def _():
        q_copies = []
        for h in range(heads):
            at = (base + h) * HS
            q_copies.append(pltpu.make_async_copy(
                q_ref.at[:, at:at + HS], q_buf.at[pl.ds(h * TOK, TOK), :], q_sems.at[h]))
            q_copies[-1].start()
        for d in range(SLOTS):
            @pl.when(d <= z)
            def _():
                for copy in slot_copies(d):
                    copy.start()

        v_buf[:, :, HS:] = jnp.ones((SLOTS, PAIR, HS), jnp.bfloat16)

        def score(t, j, n):
            keys = k_buf[pl.ds(j, n)].reshape(n * PAIR, HS)
            return lax.dot_general(
                q_buf[t * ROWS:(t + 1) * ROWS, :], keys, (((1,), (1,)), ((), ())),
                preferred_element_type=jnp.float32)

        def lane_max(s):
            top = s[:, :HS]
            for i in range(1, s.shape[1] // HS):
                top = jnp.maximum(top, s[:, i * HS:(i + 1) * HS])
            return top

        def score_first(t):
            s = score(t, 0, 1)
            row = lax.broadcasted_iota(jnp.int32, (ROWS, PAIR), 0) & (TOK - 1)
            col = lax.broadcasted_iota(jnp.int32, (ROWS, PAIR), 1)
            seen = (col <= row) | ((col >= TOK) & (x_lo == 1))
            s = jnp.where(seen, s, -1e30)
            s_buf[0] = s
            m_buf[t % 2] = lane_max(s)

        def score_block(t, j, n):
            s = score(t, j, n)
            for i in range(n):
                s_buf[j + i] = s[:, i * PAIR:(i + 1) * PAIR]
            m_buf[t % 2] = jnp.maximum(m_buf[t % 2], lane_max(s))

        def finish_max(t):
            m_buf[t % 2] = jnp.broadcast_to(m_buf[t % 2].max(axis=-1, keepdims=True), (ROWS, HS))

        def mix(t, j, n):
            wide = jnp.concatenate([m_buf[t % 2]] * (PAIR // HS), axis=1)
            p = [jnp.exp2((s_buf[j + i] - wide) * SCALE_LOG2E).astype(jnp.bfloat16) for i in range(n)]
            values = v_buf[pl.ds(j, n)].reshape(n * PAIR, 2 * HS)
            return jnp.dot(jnp.concatenate(p, axis=1), values, preferred_element_type=jnp.float32)

        def write_out(t):
            acc = acc_buf[...]
            row = (lax.broadcasted_iota(jnp.int32, (ROWS, HS), 0) & (TOK - 1)) + first
            o = jnp.where(row < length, acc[:, :HS] / acc[:, HS:], 0.0).astype(out_ref.dtype)
            for i in range(ROWS // TOK):
                h = keep + t * (ROWS // TOK) + i
                out_ref[:, h * HS:(h + 1) * HS] = o[i * TOK:(i + 1) * TOK]

        for copy in q_copies:
            copy.wait()
        tiles = heads * TOK // ROWS
        for t in range(tiles + 1):
            if t == 0:
                arrive(0)
            if t > 0:
                acc_buf[...] = mix(t - 1, 0, 1)
            if t < tiles:
                score_first(t)

            def step(j, n):
                if t == 0:
                    for i in range(n):
                        arrive(j + i)
                if t > 0:
                    acc_buf[...] += mix(t - 1, j, n)
                if t < tiles:
                    score_block(t, j, n)

            def two(i, carry):
                step(1 + 2 * i, 2)
                return carry

            lax.fori_loop(0, z // 2, two, 0)

            @pl.when(z % 2 == 1)
            def _():
                step(z, 1)

            if t < tiles:
                finish_max(t)
            if t > 0:
                write_out(t - 1)


def attention(base, heads, info, q, sources, blocks, kept=()):
    keep = base if kept else 0
    width = (keep + heads) * HS
    return pl.pallas_call(
        functools.partial(attention_kernel, base, heads, keep, sources),
        out_shape=jax.ShapeDtypeStruct((TOK, width), jnp.bfloat16),
        in_specs=[SCALARS, ANYWHERE] + [WHOLE] * len(kept) + [ANYWHERE] * len(blocks),
        out_specs=WHOLE,
        scratch_shapes=[
            pltpu.VMEM((heads * TOK, HS), jnp.bfloat16),
            pltpu.VMEM((SLOTS, PAIR, HS), jnp.bfloat16),
            pltpu.VMEM((SLOTS, PAIR, 2 * HS), jnp.bfloat16),
            pltpu.VMEM((SLOTS, ROWS, PAIR), jnp.float32),
            pltpu.VMEM((2, ROWS, HS), jnp.float32),
            pltpu.VMEM((ROWS, 2 * HS), jnp.float32),
            pltpu.SemaphoreType.DMA((SLOTS, 2, 2)),
            pltpu.SemaphoreType.DMA((heads,)),
        ],
        compiler_params=pltpu.CompilerParams(vmem_limit_bytes=VMEM_LIMIT),
        cost_estimate=pl.CostEstimate(flops=heads * 3_500_000_000, bytes_accessed=2 << 20, transcendentals=0),
        name="attention",
    )(info, q, *kept, *blocks)


def projection_kernel(places, build, info_ref, *rest):
    count = len(places)
    inputs = 8 if build else 1
    parts, rest = rest[:inputs], rest[inputs:]
    w_refs, rest = (rest[:SLOTS + 1], rest[SLOTS + 1:2 * SLOTS + 2]), rest[2 * SLOTS + 2:]
    outs, rest = rest[:count], rest[count:]
    if build:
        a_buf, w_buf, sems = rest
    else:
        (a_buf,) = parts
        w_buf, sems = rest
    z = info_ref[0]
    y = info_ref[4]
    x_hi = info_ref[5]

    def pair(place, d):
        copies = []
        for side, refs in enumerate(w_refs):
            dst, sem = w_buf.at[place, side], sems.at[place, side]
            if d == 4:
                low = refs[4].shape[0]
                copies.append(pltpu.make_async_copy(refs[4], dst.at[:low, :], sem))
                copies.append(pltpu.make_async_copy(refs[5], dst.at[low:, :], sem))
            else:
                copies.append(pltpu.make_async_copy(refs[d + (d > 4)], dst, sem))
        return copies

    for place, (r, e) in enumerate(places):
        zz = lax.rem(y + r, 4) * 2 + lax.rem(x_hi + e, 2)
        need = lax.rem(z - zz + SLOTS, SLOTS)
        for d in range(SLOTS):
            @pl.when(need == d)
            def _():
                for copy in pair(place, d):
                    copy.start()

    if build:
        att0, near1, near3, att1, mix1, mix3, top, bottom = parts
        half, cut, last = TOK // 2, att0.shape[1], att1.shape[1]
        wide = HEADS * HS
        a_buf[:TOK, :cut] = att0[...]
        a_buf[:TOK, cut:wide] = att1[...]
        a_buf[TOK:, :cut] = near1[...]
        a_buf[TOK:, cut:wide] = mix1[:TOK]
        a_buf[TOK:, wide:wide + cut] = near3[...]
        a_buf[TOK:, wide + cut:] = mix3[:TOK]
        for i in range(cut // last):
            cols = slice(wide + i * last, wide + (i + 1) * last)
            rows = slice(TOK + i * half, TOK + (i + 1) * half)
            a_buf[:half, cols] = mix1[rows]
            a_buf[half:TOK, cols] = mix3[rows]
        a_buf[:half, wide + cut:] = top[...]
        a_buf[half:TOK, wide + cut:] = bottom[...]

    for place, _ in enumerate(places):
        for copy in pair(place, 0):
            copy.wait()
        w = jnp.concatenate([w_buf[place, 0], w_buf[place, 1]], axis=1)
        out = jnp.dot(a_buf[...], w, preferred_element_type=jnp.float32)
        outs[place][...] = out.astype(jnp.bfloat16)


def projection(places, info, a_parts, weights):
    rows, cols = weights[0].shape
    count = len(places)
    build = len(a_parts) > 1
    shapes = [jax.ShapeDtypeStruct((PAIR, 2 * cols), jnp.bfloat16)] * count
    if build:
        shapes.append(jax.ShapeDtypeStruct((PAIR, rows), jnp.bfloat16))
    return pl.pallas_call(
        functools.partial(projection_kernel, places, build),
        out_shape=shapes,
        in_specs=[SCALARS] + [WHOLE] * len(a_parts) + [ANYWHERE] * len(weights),
        out_specs=[WHOLE] * len(shapes),
        scratch_shapes=[
            pltpu.VMEM((count, 2, rows, cols), jnp.bfloat16),
            pltpu.SemaphoreType.DMA((count, 2)),
        ],
        compiler_params=pltpu.CompilerParams(vmem_limit_bytes=VMEM_LIMIT),
        cost_estimate=pl.CostEstimate(
            flops=count * 800_000_000, bytes_accessed=count << 20, transcendentals=0),
        name="projection",
    )(info, *a_parts, *weights)


def assemble_kernel(info_ref, p0, p1, p2, p3, out_ref):
    x_lo = info_ref[1]
    x_hi = info_ref[5]
    g = info_ref[6]
    for rel, ref in enumerate((p0, p1, p2, p3)):
        src_lo = lax.rem(x_lo + (rel & 1), 2)
        src_hi = lax.rem(x_hi + (rel >> 1), 2)
        base = ((1 - src_lo) * 2 + src_hi) * 256
        for k in range(2):
            at = base + lax.rem(g + k, 2) * HS
            out_ref[:, pl.ds(pl.multiple_of(at, HS), HS)] = ref[:, k * HS:(k + 1) * HS]


def assemble(info, pieces):
    return pl.pallas_call(
        assemble_kernel,
        out_shape=jax.ShapeDtypeStruct((TOK, 4 * pieces[0].shape[1]), jnp.bfloat16),
        in_specs=[SCALARS] + [WHOLE] * 4,
        out_specs=WHOLE,
        compiler_params=pltpu.CompilerParams(vmem_limit_bytes=VMEM_LIMIT),
        name="assemble",
    )(info, *pieces)


def after(value, *others):
    return lax.optimization_barrier((value, *others))[0]


def local(queries, key_rows, value_rows, out_weight, lengths):
    blk = lax.axis_index("blk")
    tp = lax.axis_index("tp")
    g = lax.axis_index("grp")
    z, x_lo = blk // 2, blk % 2
    y, x_hi = tp // 2, tp % 2
    info = jnp.stack([z, x_lo, blk * TOK, lengths[0], y, x_hi, g, jnp.zeros_like(g)]).astype(jnp.int32)

    def z_shift(value, step):
        return lax.ppermute(value, "blk", [(i, (i + 2 * step) % 16) for i in range(16)])

    def y_shift(value, step):
        return lax.ppermute(value, "tp", [(i, (i + 2 * step) % 8) for i in range(8)])

    def x_flip(value, rel):
        if rel == 1:
            return lax.ppermute(value, "blk", [(i, i ^ 1) for i in range(16)])
        if rel == 2:
            return lax.ppermute(value, "tp", [(i, i ^ 1) for i in range(8)])
        return lax.ppermute(value, ("blk", "tp"), [(i, i ^ 9) for i in range(128)])

    def swap(value):
        return lax.ppermute(value, "grp", [(0, 1), (1, 0)])

    quarter = out_weight.shape[1] // 4
    keep_at, give_at = (x_hi * 2 + g) * quarter, ((1 - x_hi) * 2 + g) * quarter
    info, keep_at, give_at = lax.optimization_barrier(
        (info, keep_at.astype(jnp.uint32), give_at.astype(jnp.uint32)))

    own_kv = jnp.concatenate([key_rows[0], value_rows[0]], axis=1)
    own_kv = after(own_kv, info, keep_at, give_at)
    up1, dn1 = z_shift(own_kv, 1), z_shift(own_kv, -1)
    up2, dn2 = z_shift(up1, 1), z_shift(dn1, -1)
    up3, dn3 = z_shift(up2, 1), z_shift(dn2, -1)
    up4 = z_shift(up3, 1)
    blocks = []
    for mine in (own_kv, up1, up2, up3, up4, dn3, dn2, dn1):
        blocks += [mine, x_flip(mine, 1)]
    sources = tuple(((2 * d, 0), (2 * d + 1, 0)) for d in range(SLOTS))

    shape = (out_weight.shape[0], quarter)
    give1 = lax.dynamic_slice(out_weight, (jnp.uint32(0), keep_at), shape)
    give3 = lax.dynamic_slice(out_weight, (jnp.uint32(0), give_at), shape)
    give1, give3 = after(give1, up1), after(give3, up1)
    w0 = jnp.concatenate([x_flip(give1, 1), x_flip(give3, 3)], axis=0)
    w0 = after(w0, dn3)
    rows = w0.shape[0] // 2
    w_up1, w_dn1 = z_shift(w0, 1), z_shift(w0, -1)

    o0 = swap(w0)
    head = after(attention(0, 2, info, queries[0], sources, blocks), o0)
    w_up2, w_dn2 = z_shift(after(w_up1, head), 1), z_shift(after(w_dn1, head), -1)
    o_up1, o_dn1 = swap(w_up1), swap(w_dn1)
    att0 = attention(2, 4, info, queries[0], sources, blocks, (head,))
    att0 = after(att0, o_up1, o_dn1)
    near1, near3 = x_flip(att0, 1), x_flip(att0, 3)
    w_up3, w_dn3 = z_shift(after(w_up2, att0), 1), z_shift(after(w_dn2, att0), -1)
    o_up2, o_dn2 = swap(after(w_up2, att0)), swap(after(w_dn2, att0))
    att1 = attention(6, 2, info, after(queries[0], att0), sources, blocks)
    half, last = TOK // 2, att1.shape[1]

    def message(a, far):
        return jnp.concatenate([a] + [far[:, i:i + last] for i in range(0, far.shape[1], last)], 0)

    send1, send3 = message(att1, near3[:half]), message(att1, near1[half:])
    w_up3, w_dn3, _ = lax.optimization_barrier((w_up3, w_dn3, send3))
    w_up4, w_dn4 = z_shift(w_up3[:rows], 1), z_shift(w_dn3[rows:], -1)
    mix1, mix3, w_up4, w_dn4 = lax.optimization_barrier((x_flip(send1, 1), x_flip(send3, 3), w_up4, w_dn4))
    top, bottom, o_up4, o_dn4 = lax.optimization_barrier(
        (x_flip(mix3[:half], 1), x_flip(mix1[half:TOK], 3), swap(w_up4), swap(w_dn4)))
    a_parts = (att0, near1, near3, att1, mix1, mix3, top, bottom)

    weights = (w0, w_up1, w_up2, w_up3, w_up4, w_dn4, w_dn3, w_dn2, w_dn1,
               o0, o_up1, o_up2, swap(w_up3), o_up4, o_dn4, swap(w_dn3), o_dn2, o_dn1)

    f32 = jnp.float32
    c2s, c2f, a_full = projection(((2, 0), (2, 1)), info, a_parts, weights)
    up_2f, dn_2s = lax.optimization_barrier((y_shift(c2f, 1), y_shift(c2s, -1)))
    c1s, c3f = projection(((1, 0), (3, 1)), info, (a_full,), weights)
    up_s, dn_f = lax.optimization_barrier((y_shift(c1s, 1), y_shift(c3f, -1)))
    c1f, c3s = projection(((1, 1), (3, 0)), info, (after(a_full, c1s),), weights)
    sum_f = (c1f.astype(f32) + up_2f.astype(f32)).astype(jnp.bfloat16)
    sum_s = (c3s.astype(f32) + dn_2s.astype(f32)).astype(jnp.bfloat16)
    sum_f, sum_s = lax.optimization_barrier((sum_f, sum_s))
    up_f, dn_s = lax.optimization_barrier((y_shift(sum_f, 1), y_shift(sum_s, -1)))
    c0s, c0f = projection(((0, 0), (0, 1)), info, (after(a_full, sum_f, sum_s, up_s, dn_f),), weights)

    def total(own, up, dn, at):
        rows = slice(at, at + TOK)
        return (own[rows].astype(f32) + up[rows].astype(f32) + dn[rows].astype(f32)).astype(jnp.bfloat16)

    pieces = (
        total(c0s, up_s, dn_s, 0),
        x_flip(total(c0s, up_s, dn_s, TOK), 1),
        x_flip(total(c0f, up_f, dn_f, 0), 2),
        x_flip(total(c0f, up_f, dn_f, TOK), 3),
    )
    return assemble(info, pieces)[None]


def solution(mesh):
    in_specs = (
        P("grp", "blk", "tp"),
        P("grp", "blk", "tp"),
        P("grp", "blk", "tp"),
        P("tp", "blk"),
        P("grp"),
    )
    out_specs = P("grp", "blk", "tp")
    return jax.shard_map(local, mesh=mesh, in_specs=in_specs, out_specs=out_specs, check_vma=False)
```
